32 devices in a mesh: dp: 4 (over y, x), gx: 2 (over core), gy: 4 (over z).
Axes of the slice: x: 2, y: 2, z: 4, core: 2. Of those that a mesh axis runs over, the one named last changes fastest.
Arguments:
- inputs: bfloat16 [2, 4096, 2048], P(None, ('dp', 'gy'), 'gx'), may hold values from -6 to 6
- cotangent: bfloat16 [2, 4096, 2048], P(None, ('dp', 'gy'), 'gx'), may hold values from -6 to 6
- segments: int32 [2, 4096], P(None, 'dp'), may hold values from 0 to 3, as said below
- attention_gain: float32 [2, 2048], replicated, may hold values from 0.5 to 1.5
- query_weight: bfloat16 [2, 2048, 2048], P(None, 'gx', 'gy'), may hold values from -0.046875 to 0.046875
- key_weight: bfloat16 [2, 2048, 2048], P(None, 'gx', 'gy'), may hold values from -0.046875 to 0.046875
- value_weight: bfloat16 [2, 2048, 2048], P(None, 'gx', 'gy'), may hold values from -0.125 to 0.125
- mixing_weight: bfloat16 [2, 2048, 2048], P(None, 'gy', 'gx'), may hold values from -1 to 1
- relative_bias: float32 [2, 32, 32], replicated, may hold values from -6 to 6
- dense_gain: float32 [2, 2048], replicated, may hold values from 0.5 to 1.5
- gate_weight: bfloat16 [2, 2048, 5120], P(None, 'gx', 'gy'), may hold values from -0.125 to 0.125
- up_weight: bfloat16 [2, 2048, 5120], P(None, 'gx', 'gy'), may hold values from -0.125 to 0.125
- down_weight: bfloat16 [2, 5120, 2048], P(None, 'gy', 'gx'), may hold values from -0.078125 to 0.078125
Outputs:
- output: float32 [2, 4096, 2048], P(None, ('dp', 'gy'), 'gx')
- grad_inputs: float32 [2, 4096, 2048], P(None, ('dp', 'gy'), 'gx')
- grad_attention: float32 [2, 2048], replicated
- grad_query: float32 [2, 2048, 2048], P(None, 'gx', 'gy')
- grad_key: float32 [2, 2048, 2048], P(None, 'gx', 'gy')
- grad_value: float32 [2, 2048, 2048], P(None, 'gx', 'gy')
- grad_mixing: float32 [2, 2048, 2048], P(None, 'gy', 'gx')
- grad_relative: float32 [2, 32, 32], replicated
- grad_dense: float32 [2, 2048], replicated
- grad_gate: float32 [2, 2048, 5120], P(None, 'gx', 'gy')
- grad_up: float32 [2, 2048, 5120], P(None, 'gx', 'gy')
- grad_down: float32 [2, 5120, 2048], P(None, 'gy', 'gx')
The draws below stay inside these ranges and needn't reach their ends.
Inputs may be any that keep to these rules, and one draw needn't show every extreme that they name: `segments`: within each sequence of 1024 tokens the numbers are 1, 2 and 3 for three documents in order, never falling, each document of 65 tokens or more, and the sequence ends in 1 to 128 padding tokens numbered 0.
All inputs are finite; a program needn't handle non-finite values.
Results may differ from the reference program's by a relative error of at most 0.023.
Values may be sent and summed in bfloat16 or wider, within the bound.
No kernel may reach another device: no remote copies, remote signals or barrier semaphores. Data moves between devices by JAX's collectives and lax.ppermute only.
A program may use at most 512 MiB of HBM per device.

```python
import jax
import jax.numpy as jnp
from jax import lax

D = 2048
H = 32
DH = 64
FF = 5120
NB = 32
LAYERS = 2
MICRO = 2
LEN = 1024
TOK_ALL = 4096


def draw_segments(key, part):
    key = jax.random.fold_in(key, 11)
    length_key, pad_key = jax.random.split(key)
    seq_count = MICRO * TOK_ALL // LEN
    lengths = jax.random.randint(length_key, (seq_count, 16), LEN // 16 + 1, LEN * 3 // 8 + 1)
    bounds = jnp.cumsum(lengths, axis=1)
    places = jnp.arange(LEN, dtype=jnp.int32)
    numbers = 1 + jnp.sum((bounds[:, None, :] <= places[None, :, None]).astype(jnp.int32), axis=-1)
    numbers = jnp.minimum(numbers, 3)
    padding = jax.random.randint(pad_key, (seq_count, 1), 1, LEN // 8 + 1)
    numbers = jnp.where(places[None, :] >= LEN - padding, 0, numbers)
    return numbers.reshape(MICRO, TOK_ALL).astype(jnp.int32)


def block_scale(rng, extent, cuts, low, largest):
    factor_of, own = 1.0, jax.random.fold_in(rng, 6)
    for position, shards_of in cuts:
        draws = jnp.exp(jax.random.uniform(jax.random.fold_in(own, position), (shards_of,), jnp.float32, low / len(cuts), largest / len(cuts)))
        factor_of = factor_of * jnp.repeat(draws, extent[position] // shards_of).reshape([-1 if axis == position else 1 for axis in range(len(extent))])
    return factor_of


def scatter_about(key, extent, width, most, shards=(), held_as=jnp.bfloat16):
    drawn = jax.random.normal(key, extent, jnp.float32) * width
    if len(shards) > 0:
        drawn = block_scale(key, extent, shards, -0.22, 0.18) * drawn
    return jnp.clip(drawn, min=-most, max=most).astype(held_as)


def setup_inputs(seed: int = 0) -> dict:
    streams_of = jax.random.split(jax.random.key(seed), 14)
    inputs = scatter_about(streams_of[0], (MICRO, TOK_ALL, D), 1.0, 6.0, ((1, 16), (2, 2)))
    cotangent = scatter_about(streams_of[1], (MICRO, TOK_ALL, D), 1.0, 6.0, ((1, 16), (2, 2)))
    segments = draw_segments(jax.random.fold_in(streams_of[13], 71), 0)
    attention_gain = jnp.clip(1.0 + 0.1 * jax.random.normal(streams_of[3], (LAYERS, D), jnp.float32), 0.5, 1.5)
    query_weight = scatter_about(streams_of[4], (LAYERS, D, H * DH), (8 * D) ** -0.5, 0.046875, ((1, 2), (2, 4)))
    key_weight = scatter_about(streams_of[5], (LAYERS, D, H * DH), (8 * D) ** -0.5, 0.046875, ((1, 2), (2, 4)))
    value_weight = scatter_about(streams_of[6], (LAYERS, D, H * DH), D ** -0.5, 0.125, ((1, 2), (2, 4)))
    mixing_weight = scatter_about(streams_of[7], (LAYERS, H * DH, D), (H * DH // 64) ** -0.5, 1.0, ((1, 4), (2, 2)))
    relative_bias = scatter_about(streams_of[8], (LAYERS, NB, H), 1.0, 6.0, (), jnp.float32)
    dense_gain = jnp.clip(1.0 + 0.1 * jax.random.normal(streams_of[9], (LAYERS, D), jnp.float32), 0.5, 1.5)
    gate_weight = scatter_about(streams_of[10], (LAYERS, D, FF), D ** -0.5, 0.125, ((1, 2), (2, 4)))
    up_weight = scatter_about(streams_of[11], (LAYERS, D, FF), D ** -0.5, 0.125, ((1, 2), (2, 4)))
    down_weight = scatter_about(streams_of[12], (LAYERS, FF, D), FF ** -0.5, 0.078125, ((1, 4), (2, 2)))
    return {"inputs": inputs, "cotangent": cotangent, "segments": segments, "attention_gain": attention_gain, "query_weight": query_weight, "key_weight": key_weight, "value_weight": value_weight, "mixing_weight": mixing_weight, "relative_bias": relative_bias, "dense_gain": dense_gain, "gate_weight": gate_weight, "up_weight": up_weight, "down_weight": down_weight}


@jax.custom_vjp
def low(v):
    return lax.optimization_barrier(v.astype(jnp.bfloat16)).astype(jnp.float32)

@jax.custom_vjp
def low_back(v):
    return v

def low_keep(v):
    return (low(v), None)

def low_pass(kept, grad):
    return (grad,)

def back_keep(v):
    return (v, None)

def back_low(kept, grad):
    return (low(grad),)
low.defvjp(low_keep, low_pass)
low_back.defvjp(back_keep, back_low)
THRESHOLDS = (12, 16, 23, 32, 46, 64, 91)
HIGH = lax.Precision.HIGHEST

def bucket_of(offset):
    distance = jnp.abs(offset)
    beyond = 8 + sum(((distance >= threshold).astype(jnp.int32) for threshold in THRESHOLDS))
    within = jnp.where(distance < 8, distance, beyond)
    return (jnp.where(offset > 0, 16, 0) + within).astype(jnp.int32)

def project(values, weight):
    return jnp.einsum('std,df->stf', values, weight, precision=HIGH)

def rms_norm(hidden, gain):
    scale = lax.rsqrt(lax.optimization_barrier(jnp.mean(hidden * hidden, axis=-1, keepdims=True)) + 1e-06)
    return hidden * scale * gain

def attend_one(query, key_in, value, segment, table):
    length = query.shape[0]
    places = jnp.arange(length, dtype=jnp.int32)
    offset = places[None, :] - places[:, None]
    biases = jnp.transpose(jnp.take(table, bucket_of(offset), axis=0), (2, 0, 1))
    scores = low_back(jnp.einsum('qhd,khd->hqk', query, key_in, precision=HIGH) + biases)
    allowed = (segment[:, None] == segment[None, :]) & (segment[None, :] != 0) | (offset == 0)
    scores = jnp.where(allowed[None], scores, -1000000000.0)
    highest = lax.optimization_barrier(jnp.max(scores, axis=-1, keepdims=True))
    weights = jnp.exp(scores - highest)
    probs = weights / lax.optimization_barrier(jnp.sum(weights, axis=-1, keepdims=True))
    return jnp.einsum('hqk,khd->qhd', low(probs), value, precision=HIGH)

def forward(hidden, segment, attention_gain, query_weight, key_weight, value_weight, mixing_weight, relative_bias, dense_gain, gate_weight, up_weight, down_weight):
    seq_count = hidden.shape[0]
    for layer_index in range(LAYERS):
        normed = low(rms_norm(hidden, attention_gain[layer_index]))

        def heads_of(weight):
            return low(low_back(project(normed, weight))).reshape(seq_count, LEN, H, DH)
        query = heads_of(query_weight[layer_index])
        key_part = heads_of(key_weight[layer_index])
        value_part = heads_of(value_weight[layer_index])
        table = relative_bias[layer_index]

        def attend_items(items):
            return attend_one(items[0], items[1], items[2], items[3], table)
        mixed_heads = lax.map(jax.checkpoint(attend_items), (query, key_part, value_part, segment))
        mixed_heads = low(low_back(mixed_heads)).reshape(seq_count, LEN, H * DH)
        hidden = hidden + low_back(project(mixed_heads, mixing_weight[layer_index]))
        dense_in = low(rms_norm(hidden, dense_gain[layer_index]))
        gate_val = low_back(project(dense_in, gate_weight[layer_index]))
        up_val = low_back(project(dense_in, up_weight[layer_index]))
        activated = low(jax.nn.gelu(gate_val, approximate=True) * up_val)
        hidden = hidden + low_back(project(activated, down_weight[layer_index]))
    return hidden * (segment != 0).astype(hidden.dtype)[..., None]

def reference(inputs, cotangent, segments, attention_gain, query_weight, key_weight, value_weight, mixing_weight, relative_bias, dense_gain, gate_weight, up_weight, down_weight):
    params = tuple((item.astype(jnp.float32) for item in (attention_gain, query_weight, key_weight, value_weight, mixing_weight, relative_bias, dense_gain, gate_weight, up_weight, down_weight)))
    outputs = []
    input_grads = []
    totals = None
    for micro_index in range(MICRO):
        segment = segments[micro_index].reshape(-1, LEN)
        start = inputs[micro_index].astype(jnp.float32).reshape(-1, LEN, D)

        def whole(hidden, *weights):
            return forward(hidden, segment, *weights)
        result, pullback = jax.vjp(whole, start, *params)
        grads = pullback(cotangent[micro_index].astype(jnp.float32).reshape(-1, LEN, D))
        outputs.append(result.reshape(TOK_ALL, D))
        input_grads.append(grads[0].reshape(TOK_ALL, D))
        if totals is None:
            totals = grads[1:]
        else:
            totals = tuple((earlier + later for earlier, later in zip(totals, grads[1:])))
    return (jnp.stack(outputs), jnp.stack(input_grads), totals[0], totals[1], totals[2], totals[3], totals[4], totals[5], totals[6], totals[7], totals[8], totals[9])
```

```python
import functools

import jax
import jax.numpy as jnp
from jax import lax
from jax.experimental import pallas as pl
from jax.experimental.pallas import tpu as pltpu
from jax.sharding import PartitionSpec as P

D = 2048
H = 32
DH = 64
NB = 32
LAYERS = 2
MICRO = 2
LEN = 1024
TILE = 256
NEAR = 5
NEG = -1000000000.0
HIGH = lax.Precision.HIGHEST


def head_mask(hp, h, rows):
    lane = lax.broadcasted_iota(jnp.int32, (rows, hp*DH), 1)
    return (lane >= h*DH) & (lane < (h+1)*DH)

def pick(values, hp, h):
    if hp == 1:
        return values
    return jnp.where(head_mask(hp, h, values.shape[0]), values, jnp.zeros_like(values))

def nt(a,b): return lax.dot_general(a,b,(((1,),(1,)),((),())),preferred_element_type=jnp.float32)
def tn(a,b): return lax.dot_general(a,b,(((0,),(0,)),((),())),preferred_element_type=jnp.float32)
def nn(a,b): return lax.dot_general(a,b,(((1,),(0,)),((),())),preferred_element_type=jnp.float32)

def build_bias(hp, w_ref, bias):
    for h in range(hp):
        for d in range(NEAR):
            wide = jnp.broadcast_to(w_ref[h, d:d+1, :], (TILE, 2*TILE))
            wide = pltpu.roll(wide, 0, 1, stride=1, stride_axis=0)
            bias[h, d] = wide[:, :TILE]

def fwd_kernel(hp, span, segr, segc, q_ref, k_ref, v_ref, w_ref, o_ref, lse_ref, bias, s_ref):
    iq = pl.program_id(1)
    @pl.when(iq == 0)
    def _():
        build_bias(hp, w_ref, bias)
    lo = span[0, iq]; hi = span[1, iq]
    q = q_ref[...]
    row_seg = segr[...]
    outs = []
    lse_ref[...] = jnp.zeros_like(lse_ref)
    for h in range(hp):
        qh = pick(q, hp, h)
        def first(kc, high):
            rows = pl.ds(pl.multiple_of(kc*TILE, TILE), TILE)
            s = nt(k_ref[rows, :], qh) + bias[h, jnp.clip(kc-iq+2, 0, NEAR-1)]
            s = jnp.where(segc[rows, :] == row_seg, s, NEG)
            s_ref[rows, :] = s
            return jnp.maximum(high, jnp.max(s, axis=0, keepdims=True))
        high = lax.fori_loop(lo, hi, first, jnp.full((1, TILE), NEG, jnp.float32))
        def second(kc, carry):
            total, acc = carry
            rows = pl.ds(pl.multiple_of(kc*TILE, TILE), TILE)
            e = jnp.exp(s_ref[rows, :] - high)
            total = total + jnp.sum(e, axis=0, keepdims=True)
            acc = acc + tn(v_ref[rows, :], e.astype(jnp.bfloat16))
            return total, acc
        total, acc = lax.fori_loop(lo, hi, second, (jnp.zeros((1, TILE), jnp.float32), jnp.zeros((hp*DH, TILE), jnp.float32)))
        outs.append((acc / total)[h*DH:(h+1)*DH, :])
        lse_ref[0, h:h+1, :] = high + jnp.log(total)
    out = jnp.concatenate(outs, axis=0) if hp > 1 else outs[0]
    o_ref[...] = out.T.astype(o_ref.dtype)

def bwd_kernel(hp, span, segr, segc, q_ref, k_ref, v_ref, w_ref, o_ref, lse_ref, go_ref, gq_ref, gk_ref, gv_ref, gb_ref, bias, gbias, gk_acc, gv_acc):
    iq = pl.program_id(1)
    @pl.when(iq == 0)
    def _():
        build_bias(hp, w_ref, bias)
        gbias[...] = jnp.zeros_like(gbias)
        gk_acc[...] = jnp.zeros_like(gk_acc)
        gv_acc[...] = jnp.zeros_like(gv_acc)
    lo = span[0, iq]; hi = span[1, iq]
    q = q_ref[...]
    go = go_ref[...]
    row_seg = segr[...]
    prod = (o_ref[...].astype(jnp.float32) * go.astype(jnp.float32)).T
    outs = []
    for h in range(hp):
        qh = pick(q, hp, h)
        goh = pick(go, hp, h)
        lse = lse_ref[0, h:h+1, :]
        delta = jnp.sum(prod[h*DH:(h+1)*DH, :], axis=0, keepdims=True)
        def step(kc, acc):
            rows = pl.ds(pl.multiple_of(kc*TILE, TILE), TILE)
            near = jnp.clip(kc-iq+2, 0, NEAR-1)
            k = k_ref[rows, :]
            s = nt(k, qh) + bias[h, near]
            s = jnp.where(segc[rows, :] == row_seg, s, NEG)
            p = jnp.exp(s - lse)
            gp = nt(v_ref[rows, :], goh)
            gs = (p * (gp - delta)).astype(jnp.bfloat16)
            gv_acc[rows, :] += nn(p.astype(jnp.bfloat16), goh)
            gk_acc[rows, :] += nn(gs, qh)
            gbias[h, near] += gs.astype(jnp.float32)
            return acc + tn(k, gs)
        acc = lax.fori_loop(lo, hi, step, jnp.zeros((hp*DH, TILE), jnp.float32))
        outs.append(acc[h*DH:(h+1)*DH, :])
    out = jnp.concatenate(outs, axis=0) if hp > 1 else outs[0]
    gq_ref[...] = out.T.astype(gq_ref.dtype)
    @pl.when(iq == pl.num_programs(1) - 1)
    def _():
        gk_ref[...] = gk_acc[...].astype(gk_ref.dtype)
        gv_ref[...] = gv_acc[...].astype(gv_ref.dtype)
        gb_ref[...] = jnp.zeros_like(gb_ref)
        down = lax.broadcasted_iota(jnp.int32, (TILE, TILE), 0)
        across = lax.broadcasted_iota(jnp.int32, (TILE, TILE), 1)
        flip = (down + across == TILE - 1).astype(jnp.float32)
        for h in range(hp):
            for d in range(NEAR):
                tile = gbias[h, d]
                if 0 < d < NEAR - 1:
                    tile = lax.dot_general(flip, tile, (((1,), (0,)), ((), ())), precision=lax.Precision.HIGHEST, preferred_element_type=jnp.float32)
                wide = jnp.concatenate([tile, jnp.zeros_like(tile)], axis=1)
                if 0 < d < NEAR - 1:
                    wide = pltpu.roll(wide, 0, 1, stride=1, stride_axis=0)
                gb_ref[h, d:d+1, :] = jnp.sum(wide, axis=0, keepdims=True)

def parts_of(qkv, heads, hp):
    width = hp*DH; pairs = heads//hp
    if width % 128 == 0:
        return [(qkv, n*pairs) for n in range(3)]
    step = heads*DH
    return [(qkv[:, n*step:(n+1)*step], 0) for n in range(3)]

def attend(qkv, span, segr, segc, w):
    heads = w.shape[0]; hp = 2 if heads % 2 == 0 else 1
    width = hp*DH; pairs = heads//hp; steps = LEN//TILE
    (qa,q0),(ka,k0),(va,v0) = parts_of(qkv, heads, hp)
    grid = pltpu.PrefetchScalarGridSpec(
        num_scalar_prefetch=1, grid=(pairs, steps),
        in_specs=[
            pl.BlockSpec((1, TILE), lambda p, i, s: (0, i)),
            pl.BlockSpec((LEN, 1), lambda p, i, s: (0, 0)),
            pl.BlockSpec((TILE, width), lambda p, i, s: (i, q0+p)),
            pl.BlockSpec((LEN, width), lambda p, i, s: (0, k0+p)),
            pl.BlockSpec((LEN, width), lambda p, i, s: (0, v0+p)),
            pl.BlockSpec((hp, NEAR, 2*TILE), lambda p, i, s: (p, 0, 0)),
        ],
        out_specs=[
            pl.BlockSpec((TILE, width), lambda p, i, s: (i, p)),
            pl.BlockSpec((1, 8, TILE), lambda p, i, s: (p, 0, i)),
        ],
        scratch_shapes=[pltpu.VMEM((hp, NEAR, TILE, TILE), jnp.float32), pltpu.VMEM((LEN, TILE), jnp.float32)],
    )
    return pl.pallas_call(
        functools.partial(fwd_kernel, hp), grid_spec=grid,
        out_shape=[jax.ShapeDtypeStruct((LEN, heads*DH), jnp.bfloat16), jax.ShapeDtypeStruct((pairs, 8, LEN), jnp.float32)],
        compiler_params=pltpu.CompilerParams(vmem_limit_bytes=32*1024*1024),
        cost_estimate=pl.CostEstimate(flops=heads*LEN*LEN*DH*16, bytes_accessed=LEN*heads*DH*8, transcendentals=heads*LEN*LEN),
    )(span, segr, segc, qa, ka, va, w)

def attend_back(qkv, span, segr, segc, w, o, lse, go):
    heads = w.shape[0]; hp = 2 if heads % 2 == 0 else 1
    width = hp*DH; pairs = heads//hp; steps = LEN//TILE
    (qa,q0),(ka,k0),(va,v0) = parts_of(qkv, heads, hp)
    grid = pltpu.PrefetchScalarGridSpec(
        num_scalar_prefetch=1, grid=(pairs, steps),
        in_specs=[
            pl.BlockSpec((1, TILE), lambda p, i, s: (0, i)),
            pl.BlockSpec((LEN, 1), lambda p, i, s: (0, 0)),
            pl.BlockSpec((TILE, width), lambda p, i, s: (i, q0+p)),
            pl.BlockSpec((LEN, width), lambda p, i, s: (0, k0+p)),
            pl.BlockSpec((LEN, width), lambda p, i, s: (0, v0+p)),
            pl.BlockSpec((hp, NEAR, 2*TILE), lambda p, i, s: (p, 0, 0)),
            pl.BlockSpec((TILE, width), lambda p, i, s: (i, p)),
            pl.BlockSpec((1, 8, TILE), lambda p, i, s: (p, 0, i)),
            pl.BlockSpec((TILE, width), lambda p, i, s: (i, p)),
        ],
        out_specs=[
            pl.BlockSpec((TILE, width), lambda p, i, s: (i, p)),
            pl.BlockSpec((LEN, width), lambda p, i, s: (0, p)),
            pl.BlockSpec((LEN, width), lambda p, i, s: (0, p)),
            pl.BlockSpec((hp, 8, 2*TILE), lambda p, i, s: (p, 0, 0)),
        ],
        scratch_shapes=[pltpu.VMEM((hp, NEAR, TILE, TILE), jnp.float32)]*2 + [pltpu.VMEM((LEN, width), jnp.float32)]*2,
    )
    flat = jax.ShapeDtypeStruct((LEN, heads*DH), jnp.bfloat16)
    return pl.pallas_call(
        functools.partial(bwd_kernel, hp), grid_spec=grid,
        out_shape=[flat, flat, flat, jax.ShapeDtypeStruct((heads, 8, 2*TILE), jnp.float32)],
        compiler_params=pltpu.CompilerParams(vmem_limit_bytes=32*1024*1024),
        cost_estimate=pl.CostEstimate(flops=heads*LEN*LEN*DH*40, bytes_accessed=LEN*heads*DH*16, transcendentals=heads*LEN*LEN),
    )(span, segr, segc, qa, ka, va, w, o, lse, go)

THRESHOLDS = (12, 16, 23, 32, 46, 64, 91)
def bucket_of(offset):
    distance = jnp.abs(offset)
    beyond = 8 + sum(((distance >= threshold).astype(jnp.int32) for threshold in THRESHOLDS))
    within = jnp.where(distance < 8, distance, beyond)
    return jnp.where(offset > 0, 16, 0) + within

def near_table(back):
    place = jnp.arange(2*TILE, dtype=jnp.int32)
    turn = place - (TILE - 1) if back else jnp.where(place < TILE, place, place - 2*TILE)
    offset = TILE*(jnp.arange(NEAR, dtype=jnp.int32) - 2)[:, None] - turn[None, :]
    return (bucket_of(offset)[:, :, None] == jnp.arange(NB, dtype=jnp.int32)).astype(jnp.float32)

def segment_views(segment):
    places = jnp.arange(LEN, dtype=jnp.int32)
    own = jnp.where(segment == 0, 4 + places, segment)
    order = jnp.where(segment == 0, 4, segment).reshape(-1, TILE)
    low, high = order[:, 0], order[:, -1]
    lo = jnp.sum((high[None, :] < low[:, None]).astype(jnp.int32), axis=1)
    hi = jnp.sum((low[None, :] <= high[:, None]).astype(jnp.int32), axis=1)
    return jnp.stack((lo, hi)), own[None, :], own[:, None]


def core_swap(values):
    return lax.ppermute(values, "gx", [(0, 1), (1, 0)])


def token_gather(values):
    return lax.all_gather(values, "gy", axis=0, tiled=True)


def token_reduce(values):
    return lax.psum_scatter(values, "gy", scatter_dimension=0, tiled=True)


def dot(left, right, dims):
    return lax.dot_general(left, right, (dims, ((), ())), preferred_element_type=jnp.float32)


def row_norm(hidden):
    part = jnp.sum(hidden * hidden, axis=1)
    return lax.rsqrt((part + core_swap(part)) / D + 1e-06)


def norm_back(grad_norm, hidden, scale, gain):
    weighted = grad_norm * gain
    part = jnp.sum(weighted * hidden, axis=1)
    inner = part + core_swap(part)
    cubed = scale * scale * scale * inner / D
    grad_hidden = scale[:, None] * weighted - hidden * cubed[:, None]
    gain_grad = jnp.sum(grad_norm * hidden * scale[:, None], axis=0)
    return grad_hidden, gain_grad


def halves(weights, axis, core):
    width = weights.shape[axis] // 2
    own = lax.dynamic_slice_in_dim(weights, core * width, width, axis)
    other = lax.dynamic_slice_in_dim(weights, (1 - core) * width, width, axis)
    return own, other


def in_order(own, other, axis, core):
    return jnp.where(
        core == 0,
        jnp.concatenate((own, other), axis),
        jnp.concatenate((other, own), axis),
    )


def take_half(values, which):
    rows = values.shape[0] // 2
    return lax.dynamic_slice_in_dim(values, which * rows, rows, 0)


def batch_sum(values, place, bits):
    size = lax.axis_size("dp")
    kept = values
    trail = []
    for bit in bits:
        swap = [(i, i ^ bit) for i in range(size)]
        mine = jnp.where((place & bit) != 0, 1, 0)
        come = lax.ppermute(take_half(kept, 1 - mine), "dp", swap)
        kept = (take_half(kept, mine).astype(jnp.float32) + come.astype(jnp.float32)).astype(
            jnp.bfloat16
        )
        trail.append((swap, mine))
    for swap, mine in reversed(trail):
        kept = in_order(kept, lax.ppermute(kept, "dp", swap), 0, mine)
    return kept


def batch_sums(values, place):
    size = lax.axis_size("dp")
    bits = [1 << n for n in range(size.bit_length() - 1)]
    rows = values.shape[0] // 2
    return jnp.concatenate(
        (
            batch_sum(values[:rows], place, bits),
            batch_sum(values[rows:], place, bits[::-1]),
        ),
        0,
    )


def small_sum(values):
    for axis in ("gx", "gy", "dp"):
        size = lax.axis_size(axis)
        bit = 1
        while bit < size:
            values = values + lax.ppermute(values, axis, [(i, i ^ bit) for i in range(size)])
            bit *= 2
    return values


def body(
    inputs,
    cotangent,
    segments,
    attention_gain,
    query_weight,
    key_weight,
    value_weight,
    mixing_weight,
    relative_bias,
    dense_gain,
    gate_weight,
    up_weight,
    down_weight,
):
    core = lax.axis_index("gx")
    block = lax.axis_index("gy")
    place = lax.axis_index("dp")
    row_count = inputs.shape[1]
    col_count = inputs.shape[2]
    col_start = core * col_count
    heads_dev = query_weight.shape[2] // (2 * DH)
    head_start = (block * 2 + core) * heads_dev
    hidden_dev = gate_weight.shape[2] // 2
    bf16 = jnp.bfloat16
    ahead = near_table(False)
    behind = near_table(True)
    layers = []
    for layer in range(LAYERS):
        qs = halves(query_weight[layer], 1, core)
        ks = halves(key_weight[layer], 1, core)
        vs = halves(value_weight[layer], 1, core)
        gs = halves(gate_weight[layer], 1, core)
        us = halves(up_weight[layer], 1, core)
        table = lax.dynamic_slice_in_dim(relative_bias[layer], head_start, heads_dev, 1)
        layers.append(
            dict(
                qkv=[jnp.concatenate((qs[n], ks[n], vs[n]), 1) for n in range(2)],
                gu=[jnp.concatenate((gs[n], us[n]), 1) for n in range(2)],
                mix=halves(mixing_weight[layer], 0, core),
                down=halves(down_weight[layer], 0, core),
                bias=jnp.einsum("dcb,bh->hdc", ahead, table, precision=HIGH),
                gain1=lax.dynamic_slice_in_dim(attention_gain[layer], col_start, col_count),
                gain2=lax.dynamic_slice_in_dim(dense_gain[layer], col_start, col_count),
            )
        )
    acc = [dict() for _ in range(LAYERS)]

    def add(layer, name, value):
        have = acc[layer].get(name)
        acc[layer][name] = value if have is None else have + value

    NN = ((1,), (0,))
    NT = ((1,), (1,))
    TN = ((0,), (0,))
    micros = []
    for micro in range(MICRO):
        seg_all = segments[micro]
        row_segs = lax.dynamic_slice_in_dim(seg_all, block * row_count, row_count)
        keep = (row_segs != 0).astype(jnp.float32)[:, None]
        views = segment_views(seg_all)
        hidden = inputs[micro].astype(jnp.float32)
        saved = []
        for layer in range(LAYERS):
            w = layers[layer]
            scale1 = row_norm(hidden)
            normed = token_gather((hidden * scale1[:, None] * w["gain1"]).astype(bf16))
            come = core_swap(dot(normed, w["qkv"][1], NN).astype(bf16))
            qkv = (dot(normed, w["qkv"][0], NN) + come.astype(jnp.float32)).astype(bf16)
            mixed, lse = attend(qkv, *views, w["bias"])
            mixed_other = core_swap(mixed)
            branch = dot(mixed, w["mix"][0], NN) + dot(mixed_other, w["mix"][1], NN)
            middle = hidden + token_reduce(branch.astype(bf16)).astype(jnp.float32)
            scale2 = row_norm(middle)
            dense = token_gather((middle * scale2[:, None] * w["gain2"]).astype(bf16))
            come = core_swap(dot(dense, w["gu"][1], NN).astype(bf16))
            gate_up = dot(dense, w["gu"][0], NN) + come.astype(jnp.float32)
            active = (
                jax.nn.gelu(gate_up[:, :hidden_dev], approximate=True) * gate_up[:, hidden_dev:]
            ).astype(bf16)
            active_other = core_swap(active)
            out = dot(active, w["down"][0], NN) + dot(active_other, w["down"][1], NN)
            last = middle + token_reduce(out.astype(bf16)).astype(jnp.float32)
            saved.append(
                (
                    hidden,
                    scale1,
                    normed,
                    qkv,
                    lse,
                    mixed,
                    mixed_other,
                    middle,
                    scale2,
                    dense,
                    gate_up.astype(bf16),
                    active,
                    active_other,
                )
            )
            hidden = last
        micros.append((keep, views, saved, hidden))
    outputs = [hidden * keep for keep, _, _, hidden in micros]
    grads = [cotangent[n].astype(jnp.float32) * micros[n][0] for n in range(MICRO)]
    results = [None] * LAYERS
    for layer in reversed(range(LAYERS)):
        w = layers[layer]
        for micro in range(MICRO):
            keep, views, saved, _ = micros[micro]
            (
                hidden,
                scale1,
                normed,
                qkv,
                lse,
                mixed,
                mixed_other,
                middle,
                scale2,
                dense,
                gate_up,
                active,
                active_other,
            ) = saved[layer]
            grad = grads[micro]
            grad_out = token_gather(grad.astype(bf16))
            come = core_swap(dot(grad_out, w["down"][1], NT).astype(bf16))
            grad_active = dot(grad_out, w["down"][0], NT) + come.astype(jnp.float32)
            gate = gate_up[:, :hidden_dev].astype(jnp.float32)
            up = gate_up[:, hidden_dev:].astype(jnp.float32)
            _, pull = jax.vjp(lambda a, b: jax.nn.gelu(a, approximate=True) * b, gate, up)
            pair = jnp.concatenate(pull(grad_active), 1).astype(bf16)
            pair_other = core_swap(pair)
            grad_dense = dot(pair, w["gu"][0], NT) + dot(pair_other, w["gu"][1], NT)
            grad_dense = token_reduce(grad_dense.astype(bf16)).astype(jnp.float32)
            add(layer, "down0", dot(active, grad_out, TN))
            add(layer, "down1", dot(active_other, grad_out, TN))
            add(layer, "gu0", dot(dense, pair, TN))
            add(layer, "gu1", dot(dense, pair_other, TN))
            grad_norm, gain_part = norm_back(grad_dense, middle, scale2, w["gain2"])
            add(layer, "gain2", gain_part)
            grad_mid = grad + grad_norm
            grad_out = token_gather(grad_mid.astype(bf16))
            come = core_swap(dot(grad_out, w["mix"][1], NT).astype(bf16))
            grad_mixed = (dot(grad_out, w["mix"][0], NT) + come.astype(jnp.float32)).astype(bf16)
            gq, gk, gv, gb = attend_back(qkv, *views, w["bias"], mixed, lse, grad_mixed)
            add(layer, "bias", gb)
            triple = jnp.concatenate((gq, gk, gv), 1)
            triple_other = core_swap(triple)
            grad_normed = dot(triple, w["qkv"][0], NT) + dot(triple_other, w["qkv"][1], NT)
            grad_normed = token_reduce(grad_normed.astype(bf16)).astype(jnp.float32)
            add(layer, "mix0", dot(mixed, grad_out, TN))
            add(layer, "mix1", dot(mixed_other, grad_out, TN))
            add(layer, "qkv0", dot(normed, triple, TN))
            add(layer, "qkv1", dot(normed, triple_other, TN))
            grad_norm, gain_part = norm_back(grad_normed, hidden, scale1, w["gain1"])
            add(layer, "gain1", gain_part)
            grads[micro] = grad_mid + grad_norm
        have = acc[layer]
        for name in ("down", "gu", "mix", "qkv"):
            have[name] = [
                batch_sums(have[name + str(n)].astype(bf16), place).astype(jnp.float32)
                for n in range(2)
            ]

    def columns(name, count):
        result = [[] for _ in range(count)]
        for layer in range(LAYERS):
            own, other = acc[layer][name]
            width = own.shape[1] // count
            for n in range(count):
                cut = slice(n * width, (n + 1) * width)
                result[n].append(in_order(own[:, cut], other[:, cut], 1, core))
        return [jnp.stack(item) for item in result]

    grad_query, grad_key, grad_value = columns("qkv", 3)
    grad_gate, grad_up = columns("gu", 2)
    grad_mixing = jnp.stack([in_order(*acc[n]["mix"], 0, core) for n in range(LAYERS)])
    grad_down = jnp.stack([in_order(*acc[n]["down"], 0, core) for n in range(LAYERS)])
    gain = jnp.stack([acc[n][name] for name in ("gain1", "gain2") for n in range(LAYERS)])
    gain = lax.dynamic_update_slice_in_dim(
        jnp.zeros((2 * LAYERS, D), jnp.float32), gain, col_start, 1
    )
    bias = jnp.stack([acc[n]["bias"][:, :NEAR] for n in range(LAYERS)])
    bias = jnp.einsum("lhdc,dcb->lbh", bias, behind, precision=HIGH)
    bias = lax.dynamic_update_slice_in_dim(
        jnp.zeros((LAYERS, NB, H), jnp.float32), bias, head_start, 2
    )
    small = small_sum(jnp.concatenate((gain.reshape(-1, 128), bias.reshape(-1, 128)), 0))
    split = gain.size // 128
    gain = small[:split].reshape(gain.shape)
    bias = small[split:].reshape(bias.shape)
    return (
        jnp.stack(outputs),
        jnp.stack(grads),
        gain[:LAYERS],
        grad_query,
        grad_key,
        grad_value,
        grad_mixing,
        bias,
        gain[LAYERS:],
        grad_gate,
        grad_up,
        grad_down,
    )


def solution(mesh):
    tokens = P(None, ("dp", "gy"), "gx")
    wide = P(None, "gx", "gy")
    tall = P(None, "gy", "gx")
    return jax.shard_map(
        body,
        mesh=mesh,
        in_specs=(
            tokens,
            tokens,
            P(None, "dp"),
            P(),
            wide,
            wide,
            wide,
            tall,
            P(),
            P(),
            wide,
            wide,
            tall,
        ),
        out_specs=(tokens, tokens, P(), wide, wide, wide, tall, P(), P(), wide, wide, tall),
        check_vma=False,
    )
```

```python
import functools

import jax
import jax.numpy as jnp
from jax import lax
from jax.experimental import pallas as pl
from jax.experimental.pallas import tpu as pltpu
from jax.sharding import PartitionSpec as P

D = 2048
H = 32
DH = 64
NB = 32
LAYERS = 2
MICRO = 2
LEN = 1024
TILE = 256
NEAR = 5
NEG = -1000000000.0
HIGH = lax.Precision.HIGHEST
ROWS = 256
GELU_A = 0.7978845608028654
GELU_B = 0.044715


def lanes_of(head, heads):
    wide = min(2, heads) * DH
    start = head * DH // wide * wide
    return slice(start, start + wide)


def pick(values, head, heads):
    values = values[:, lanes_of(head, heads)]
    if heads == 1:
        return values
    lane = lax.broadcasted_iota(jnp.int32, values.shape, 1)
    return jnp.where((lane // DH) == head % 2, values, jnp.zeros_like(values))


def join(rows, heads):
    if heads == 1:
        return rows[0]
    return jnp.concatenate([rows[h][h % 2 * DH : h % 2 * DH + DH] for h in range(heads)], 0)


def nt(a, b):
    return lax.dot_general(a, b, (((1,), (1,)), ((), ())), preferred_element_type=jnp.float32)


def nn(a, b):
    return lax.dot_general(a, b, (((1,), (0,)), ((), ())), preferred_element_type=jnp.float32)


def build_bias(heads, w_ref, bias):
    for h in range(heads):
        for d in range(NEAR):
            wide = jnp.broadcast_to(w_ref[h, d : d + 1, :], (TILE, 2 * TILE))
            if 0 < d < NEAR - 1:
                wide = pltpu.roll(wide, 0, 1, stride=1, stride_axis=0)
            bias[h, d] = wide[:, :TILE]


def fwd_kernel(heads, span, segr, segc, q_ref, k_ref, v_ref, w_ref, o_ref, lse_ref, bias, turned):
    iq = pl.program_id(0)

    @pl.when(iq == 0)
    def _():
        build_bias(heads, w_ref, bias)
        turned[...] = v_ref[...].T

    q = q_ref[...]
    row_seg = segr[...]
    queries = [pick(q, h, heads) for h in range(heads)]
    wide = min(2, heads) * DH

    def step(kc, carry):
        rows = pl.ds(pl.multiple_of(kc * TILE, TILE), TILE)
        near = jnp.clip(kc - iq + 2, 0, NEAR - 1)
        allowed = segc[rows, :] == row_seg
        k = k_ref[rows, :]
        out = []
        for h in range(heads):
            high, total, acc = carry[h]
            s = nt(k[:, lanes_of(h, heads)], queries[h]) + bias[h, near]
            s = jnp.where(allowed, s, NEG)
            top = jnp.maximum(high, jnp.max(s, axis=0, keepdims=True))
            scale = jnp.exp(high - top)
            e = jnp.exp(s - top)
            total = total * scale + jnp.sum(e, axis=0, keepdims=True)
            acc = acc * scale + nn(turned[lanes_of(h, heads), rows], e.astype(jnp.bfloat16))
            out.append((top, total, acc))
        return tuple(out)

    start = (
        jnp.full((1, TILE), 2 * NEG, jnp.float32),
        jnp.zeros((1, TILE), jnp.float32),
        jnp.zeros((wide, TILE), jnp.float32),
    )
    done = lax.fori_loop(span[0, iq], span[1, iq], step, (start,) * heads)
    lse_ref[...] = jnp.zeros_like(lse_ref)
    for h in range(heads):
        lse_ref[h : h + 1, :] = done[h][0] + jnp.log(done[h][1])
    out = join([acc / total for _, total, acc in done], heads)
    o_ref[...] = out.T.astype(o_ref.dtype)


def bwd_kernel(
    heads,
    span,
    segr,
    segc,
    q_ref,
    k_ref,
    v_ref,
    w_ref,
    o_ref,
    lse_ref,
    go_ref,
    gq_ref,
    gk_ref,
    gv_ref,
    gb_ref,
    bias,
    gbias,
    gk_acc,
    gv_acc,
    turned,
):
    iq = pl.program_id(0)

    @pl.when(iq == 0)
    def _():
        build_bias(heads, w_ref, bias)
        turned[...] = k_ref[...].T
        gbias[...] = jnp.zeros_like(gbias)
        gk_acc[...] = jnp.zeros_like(gk_acc)
        gv_acc[...] = jnp.zeros_like(gv_acc)

    q = q_ref[...]
    go = go_ref[...]
    row_seg = segr[...]
    prod = (o_ref[...].astype(jnp.float32) * go.astype(jnp.float32)).T
    queries = [pick(q, h, heads) for h in range(heads)]
    outs = [pick(go, h, heads) for h in range(heads)]
    lse = [lse_ref[h : h + 1, :] for h in range(heads)]
    delta = [
        jnp.sum(prod[h * DH : (h + 1) * DH, :], axis=0, keepdims=True) for h in range(heads)
    ]
    wide = min(2, heads) * DH

    def step(kc, carry):
        rows = pl.ds(pl.multiple_of(kc * TILE, TILE), TILE)
        near = jnp.clip(kc - iq + 2, 0, NEAR - 1)
        allowed = segc[rows, :] == row_seg
        k = k_ref[rows, :]
        v = v_ref[rows, :]
        result = []
        for h in range(heads):
            lanes = lanes_of(h, heads)
            s = nt(k[:, lanes], queries[h]) + bias[h, near]
            s = jnp.where(allowed, s, NEG)
            p = jnp.exp(s - lse[h])
            gp = nt(v[:, lanes], outs[h])
            gs = (p * (gp - delta[h])).astype(jnp.bfloat16)
            gv_acc[rows, lanes] += nn(p.astype(jnp.bfloat16), outs[h])
            gk_acc[rows, lanes] += nn(gs, queries[h])
            gbias[h, near] += gs.astype(jnp.float32)
            result.append(carry[h] + nn(turned[lanes, rows], gs))
        return tuple(result)

    start = (jnp.zeros((wide, TILE), jnp.float32),) * heads
    done = lax.fori_loop(span[0, iq], span[1, iq], step, start)
    gq_ref[...] = join(done, heads).T.astype(gq_ref.dtype)

    @pl.when(iq == pl.num_programs(0) - 1)
    def _():
        gk_ref[...] = gk_acc[...].astype(gk_ref.dtype)
        gv_ref[...] = gv_acc[...].astype(gv_ref.dtype)
        gb_ref[...] = jnp.zeros_like(gb_ref)
        down = lax.broadcasted_iota(jnp.int32, (TILE, TILE), 0)
        across = lax.broadcasted_iota(jnp.int32, (TILE, TILE), 1)
        flip = (down + across == TILE - 1).astype(jnp.float32)
        for h in range(heads):
            for d in range(NEAR):
                tile = gbias[h, d]
                if 0 < d < NEAR - 1:
                    tile = lax.dot_general(
                        flip,
                        tile,
                        (((1,), (0,)), ((), ())),
                        precision=HIGH,
                        preferred_element_type=jnp.float32,
                    )
                wide = jnp.concatenate([tile, jnp.zeros_like(tile)], axis=1)
                if 0 < d < NEAR - 1:
                    wide = pltpu.roll(wide, 0, 1, stride=1, stride_axis=0)
                gb_ref[h, d : d + 1, :] = jnp.sum(wide, axis=0, keepdims=True)


def parts_of(qkv, width):
    if width % 128 == 0:
        return [(qkv, n) for n in range(3)]
    return [(qkv[:, n * width : (n + 1) * width], 0) for n in range(3)]


def seen_specs(qkv, heads):
    width = heads * DH
    (qa, q0), (ka, k0), (va, v0) = parts_of(qkv, width)
    specs = [
        pl.BlockSpec((1, TILE), lambda i, s: (0, i)),
        pl.BlockSpec((LEN, 1), lambda i, s: (0, 0)),
        pl.BlockSpec((TILE, width), lambda i, s: (i, q0)),
        pl.BlockSpec((LEN, width), lambda i, s: (0, k0)),
        pl.BlockSpec((LEN, width), lambda i, s: (0, v0)),
        pl.BlockSpec((heads, NEAR, 2 * TILE), lambda i, s: (0, 0, 0)),
    ]
    return specs, (qa, ka, va)


def attend(qkv, span, segr, segc, w):
    heads = w.shape[0]
    width = heads * DH
    specs, parts = seen_specs(qkv, heads)
    tile = pl.BlockSpec((TILE, width), lambda i, s: (i, 0))
    sums = pl.BlockSpec((8, TILE), lambda i, s: (0, i))
    grid = pltpu.PrefetchScalarGridSpec(
        num_scalar_prefetch=1,
        grid=(LEN // TILE,),
        in_specs=specs,
        out_specs=[tile, sums],
        scratch_shapes=[
            pltpu.VMEM((heads, NEAR, TILE, TILE), jnp.float32),
            pltpu.VMEM((width, LEN), jnp.bfloat16),
        ],
    )
    return pl.pallas_call(
        functools.partial(fwd_kernel, heads),
        grid_spec=grid,
        out_shape=[
            jax.ShapeDtypeStruct((LEN, width), jnp.bfloat16),
            jax.ShapeDtypeStruct((8, LEN), jnp.float32),
        ],
        compiler_params=pltpu.CompilerParams(vmem_limit_bytes=40 * 1024 * 1024),
        cost_estimate=pl.CostEstimate(flops=0, bytes_accessed=0, transcendentals=0),
    )(span, segr, segc, *parts, w)


def attend_back(qkv, span, segr, segc, w, o, lse, go):
    heads = w.shape[0]
    width = heads * DH
    specs, parts = seen_specs(qkv, heads)
    tile = pl.BlockSpec((TILE, width), lambda i, s: (i, 0))
    sums = pl.BlockSpec((8, TILE), lambda i, s: (0, i))
    whole = pl.BlockSpec((LEN, width), lambda i, s: (0, 0))
    grid = pltpu.PrefetchScalarGridSpec(
        num_scalar_prefetch=1,
        grid=(LEN // TILE,),
        in_specs=specs + [tile, sums, tile],
        out_specs=[tile, whole, whole, pl.BlockSpec((heads, 8, 2 * TILE), lambda i, s: (0, 0, 0))],
        scratch_shapes=[pltpu.VMEM((heads, NEAR, TILE, TILE), jnp.float32)] * 2
        + [pltpu.VMEM((LEN, width), jnp.float32)] * 2
        + [pltpu.VMEM((width, LEN), jnp.bfloat16)],
    )
    flat = jax.ShapeDtypeStruct((LEN, width), jnp.bfloat16)
    return pl.pallas_call(
        functools.partial(bwd_kernel, heads),
        grid_spec=grid,
        out_shape=[flat, flat, flat, jax.ShapeDtypeStruct((heads, 8, 2 * TILE), jnp.float32)],
        compiler_params=pltpu.CompilerParams(vmem_limit_bytes=40 * 1024 * 1024),
        cost_estimate=pl.CostEstimate(flops=0, bytes_accessed=0, transcendentals=0),
    )(span, segr, segc, *parts, w, o, lse, go)


THRESHOLDS = (12, 16, 23, 32, 46, 64, 91)
def bucket_of(offset):
    distance = jnp.abs(offset)
    beyond = 8 + sum(((distance >= threshold).astype(jnp.int32) for threshold in THRESHOLDS))
    within = jnp.where(distance < 8, distance, beyond)
    return jnp.where(offset > 0, 16, 0) + within

def near_table(back):
    place = jnp.arange(2*TILE, dtype=jnp.int32)
    turn = place - (TILE - 1) if back else jnp.where(place < TILE, place, place - 2*TILE)
    offset = TILE*(jnp.arange(NEAR, dtype=jnp.int32) - 2)[:, None] - turn[None, :]
    return (bucket_of(offset)[:, :, None] == jnp.arange(NB, dtype=jnp.int32)).astype(jnp.float32)

def segment_views(segment):
    places = jnp.arange(LEN, dtype=jnp.int32)
    own = jnp.where(segment == 0, 4 + places, segment)
    order = jnp.where(segment == 0, 4, segment).reshape(-1, TILE)
    low, high = order[:, 0], order[:, -1]
    lo = jnp.sum((high[None, :] < low[:, None]).astype(jnp.int32), axis=1)
    hi = jnp.sum((low[None, :] <= high[:, None]).astype(jnp.int32), axis=1)
    return jnp.stack((lo, hi)), own[None, :], own[:, None]


NN = ((1,), (0,))
NT = ((1,), (1,))
TN = ((0,), (0,))
BF = jnp.bfloat16
F32 = jnp.float32


def core_swap(values):
    return lax.ppermute(values, "gx", [(0, 1), (1, 0)])


def token_gather(values):
    return lax.all_gather(values, "gy", axis=0, tiled=True)


def token_reduce(values):
    return lax.psum_scatter(values, "gy", scatter_dimension=0, tiled=True).astype(F32)


def shifted(values, step):
    size = lax.axis_size("gy")
    return lax.ppermute(values, "gy", [(n, (n + step) % size) for n in range(size)])


def dot(left, right, dims):
    return lax.dot_general(left, right, (dims, ((), ())), preferred_element_type=F32)


def rows_kernel(dims, count, extras, finish, *refs):
    total = None
    for n in range(count):
        part = dot(refs[n][...], refs[count + n][...], dims)
        total = part if total is None else total + part
    inner = 2 * count + extras
    finish(total, [ref[...] for ref in refs[2 * count : inner]], refs[inner:])


def keep_rounded(total, extras, outs):
    outs[0][...] = total.astype(BF)


def add_rounded(total, extras, outs):
    outs[0][...] = (total + extras[0].astype(F32)).astype(BF)


def gelu_parts(gate):
    inner = GELU_A * (gate + GELU_B * gate * gate * gate)
    half = 0.5 * (1.0 + jnp.tanh(inner))
    return half, gate * half


def gate_rounded(total, extras, outs):
    total = total + extras[0].astype(F32)
    width = total.shape[1] // 2
    gate, up = total[:, :width], total[:, width:]
    outs[0][...] = total.astype(BF)
    outs[1][...] = (gelu_parts(gate)[1] * up).astype(BF)


def gate_back_rounded(total, extras, outs):
    grad = total + extras[0].astype(F32)
    width = grad.shape[1]
    gate = extras[1][:, :width].astype(F32)
    up = extras[1][:, width:].astype(F32)
    half, value = gelu_parts(gate)
    slope = half + 2.0 * gate * half * (1.0 - half) * GELU_A * (1.0 + 3.0 * GELU_B * gate * gate)
    outs[0][:, :width] = (grad * up * slope).astype(BF)
    outs[0][:, width:] = (grad * value).astype(BF)


def rows_dot(parts, weights, dims, finish=keep_rounded, extras=(), widths=None):
    rows = parts[0].shape[0]
    if widths is None:
        widths = (weights[0].shape[1 - dims[1][0]],)
    outs = [jax.ShapeDtypeStruct((rows, width), BF) for width in widths]
    if not all(item.shape[1] % 128 == 0 for item in (*parts, *weights, *extras, *outs)):
        return plain_dot(parts, weights, dims, finish, extras, outs)
    tall = min(rows, ROWS)

    def sliced(item):
        return pl.BlockSpec((tall, item.shape[1]), lambda i: (i, 0))

    def whole(item):
        return pl.BlockSpec(item.shape, lambda i: (0, 0))

    result = pl.pallas_call(
        functools.partial(rows_kernel, dims, len(parts), len(extras), finish),
        grid=(rows // tall,),
        in_specs=[sliced(item) for item in parts]
        + [whole(item) for item in weights]
        + [sliced(item) for item in extras],
        out_specs=[sliced(item) for item in outs],
        out_shape=outs,
        compiler_params=pltpu.CompilerParams(vmem_limit_bytes=40 * 1024 * 1024),
        cost_estimate=pl.CostEstimate(flops=0, bytes_accessed=0, transcendentals=0),
    )(*parts, *weights, *extras)
    return result[0] if len(outs) == 1 else result


class Holder:
    def __init__(self, shape):
        self.value = jnp.zeros(shape.shape, shape.dtype)

    def __setitem__(self, place, value):
        self.value = value if place is Ellipsis else self.value.at[place].set(value)


def plain_dot(parts, weights, dims, finish, extras, outs):
    total = sum(dot(part, weight, dims) for part, weight in zip(parts, weights))
    held = [Holder(item) for item in outs]
    finish(total, extras, held)
    return held[0].value if len(held) == 1 else [item.value for item in held]


def row_norm(hidden):
    part = jnp.sum(hidden * hidden, axis=1)
    return lax.rsqrt((part + core_swap(part)) / D + 1e-06)


def norm_back(grad_norm, hidden, scale, gain):
    weighted = grad_norm * gain
    part = jnp.sum(weighted * hidden, axis=1)
    inner = part + core_swap(part)
    cubed = scale * scale * scale * inner / D
    grad_hidden = scale[:, None] * weighted - hidden * cubed[:, None]
    gain_grad = jnp.sum(grad_norm * hidden * scale[:, None], axis=0)
    return grad_hidden, gain_grad


def halves(weights, axis, core):
    width = weights.shape[axis] // 2
    own = lax.dynamic_slice_in_dim(weights, core * width, width, axis)
    other = lax.dynamic_slice_in_dim(weights, (1 - core) * width, width, axis)
    return own, other


def in_order(own, other, core, axis):
    return jnp.where(
        core == 0,
        jnp.concatenate((own, other), axis),
        jnp.concatenate((other, own), axis),
    )


def paired(*weights):
    cut = [jnp.split(item, 2, axis=1) for item in weights]
    return jnp.concatenate([item[n] for n in range(2) for item in cut], 1)


def unpaired(values, count):
    cut = jnp.split(values, 2 * count, axis=1)
    return [jnp.concatenate((cut[n], cut[count + n]), 1) for n in range(count)]


def link_swap(values, bits):
    size = lax.axis_size("dp")
    pairs = [(n * 2 + c, (n ^ bits[c]) * 2 + c) for n in range(size) for c in range(2)]
    return lax.ppermute(values, ("dp", "gx"), pairs)


def take_half(values, which):
    rows = values.shape[0] // 2
    return lax.dynamic_slice_in_dim(values, which * rows, rows, 0)


def stack_half(own, other, which):
    return jnp.where(
        which == 0,
        jnp.concatenate((own, other), 0),
        jnp.concatenate((other, own), 0),
    )


def batch_steps(place, core):
    size = lax.axis_size("dp")
    bits = [1 << n for n in range(size.bit_length() - 1)]
    steps = []
    for first, second in zip(bits, bits[::-1]):
        bit = jnp.where(core == 0, first, second)
        steps.append(((first, second), jnp.where((place & bit) != 0, 1, 0)))
    return steps


def settle_kernel(core_cut, count, place, own_ref, other_ref, *refs):
    outs = refs[-count:]
    half = pl.program_id(0)

    def store(values, core):
        width = values.shape[1] // (2 * count)
        for n in range(count):
            for part in range(2):
                start = (part * count + n) * width
                spot = (part ^ core) * width
                outs[n][0, :, spot : spot + width] = values[:, start : start + width].astype(F32)

    for source, ref in enumerate((own_ref, other_ref)):

        @pl.when((half ^ place[0]) == source)
        def _():
            if not core_cut:
                outs[0][0] = ref[...].astype(F32)
            for core in range(2 if core_cut else 0):

                @pl.when(place[1] == core)
                def _():
                    store(ref[...], core)


def settle(own, other, flag, core, layer, base, core_cut, targets, shapes):
    rows, width = own.shape
    whole = pl.BlockSpec((rows, width), lambda i, s: (0, 0))
    grid = pltpu.PrefetchScalarGridSpec(
        num_scalar_prefetch=1,
        grid=(2,),
        in_specs=[whole, whole] + [pl.BlockSpec(memory_space=pl.ANY)] * len(targets),
        out_specs=[
            pl.BlockSpec((1, rows, item.shape[2]), lambda i, s: (layer, base + i, 0))
            for item in shapes
        ],
    )
    return pl.pallas_call(
        functools.partial(settle_kernel, core_cut, len(shapes)),
        grid_spec=grid,
        out_shape=shapes,
        input_output_aliases={3 + n: n for n in range(len(targets))},
        compiler_params=pltpu.CompilerParams(vmem_limit_bytes=40 * 1024 * 1024),
        cost_estimate=pl.CostEstimate(flops=0, bytes_accessed=0, transcendentals=0),
    )(jnp.stack((flag, core)).astype(jnp.int32), own, other, *targets)


def axis_sum(values, axis):
    size = lax.axis_size(axis)

    def swapped(item, bits):
        return lax.ppermute(item, axis, [(n, n ^ bits) for n in range(size)])

    if size == 4:
        one, two, three = (swapped(values, bits) for bits in (1, 2, 3))
        return (values + one) + (two + three)
    bit = 1
    while bit < size:
        values = values + swapped(values, bit)
        bit *= 2
    return values


class Order:
    def __init__(self):
        self.last = None

    def enter(self, *values):
        if self.last is None:
            return values
        return lax.optimization_barrier((*values, self.last))[:-1]

    def leave(self, value):
        self.last = value


def body(
    inputs,
    cotangent,
    segments,
    attention_gain,
    query_weight,
    key_weight,
    value_weight,
    mixing_weight,
    relative_bias,
    dense_gain,
    gate_weight,
    up_weight,
    down_weight,
):
    core = lax.axis_index("gx")
    block = lax.axis_index("gy")
    place = lax.axis_index("dp")
    row_count = inputs.shape[1]
    col_count = inputs.shape[2]
    col_start = core * col_count
    heads_dev = query_weight.shape[2] // (2 * DH)
    head_start = (block * 2 + core) * heads_dev
    hidden_dev = gate_weight.shape[2] // 2
    ahead = near_table(False)
    behind = near_table(True)
    steps = batch_steps(place, core)
    order = Order()
    later = []
    flows = []
    summed = []
    ends = []
    results = {}
    tidy = hidden_dev % 128 == 0 and (heads_dev * DH) % 128 == 0
    shapes = [
        [jax.ShapeDtypeStruct(item.shape, F32) for item in group]
        for group in (
            (query_weight, key_weight, value_weight),
            (gate_weight, up_weight),
            (mixing_weight,),
            (down_weight,),
        )
    ]
    layers = []
    for layer in range(LAYERS):
        qkv = paired(query_weight[layer], key_weight[layer], value_weight[layer])
        gu = paired(gate_weight[layer], up_weight[layer])
        table = lax.dynamic_slice_in_dim(relative_bias[layer], head_start, heads_dev, 1)
        layers.append(
            dict(
                qkv_half=halves(qkv, 1, core),
                gu_half=halves(gu, 1, core),
                mix_half=halves(mixing_weight[layer], 0, core),
                down_half=halves(down_weight[layer], 0, core),
                bias=jnp.einsum("dcb,bh->hdc", ahead, table, precision=HIGH),
                gain1=lax.dynamic_slice_in_dim(attention_gain[layer], col_start, col_count),
                gain2=lax.dynamic_slice_in_dim(dense_gain[layer], col_start, col_count),
            )
        )
    acc = [dict() for _ in range(LAYERS)]

    def add(layer, name, value):
        have = acc[layer].get(name)
        acc[layer][name] = value if have is None else have + value

    def batch_flow(layer, name, kept, start):
        axis = 0 if name in ("down", "mix") else 1
        rows = kept.shape[0]
        for bits, mine in steps:
            (kept,) = order.enter(kept)
            send = take_half(kept, 1 - mine)
            order.leave(send)
            come = link_swap(send, bits)
            yield
            come, kept = order.enter(come, kept)
            kept = (take_half(kept, mine).astype(F32) + come.astype(F32)).astype(BF)
            order.leave(kept)
        for bits, mine in reversed(steps[1:]):
            come = link_swap(kept, bits)
            yield
            come, kept = order.enter(come, kept)
            kept = stack_half(kept, come, mine)
            order.leave(kept)
        bits, mine = steps[0]
        come = link_swap(kept, bits)
        yield
        come, kept = order.enter(come, kept)
        if tidy:
            group = ("qkv", "gu", "mix", "down").index(name)
            flag = (mine ^ core) if axis == 0 else mine
            base = start // (rows // 2)
            targets = results.get(name, [])
            results[name] = settle(
                kept, come, flag, core, layer, base, axis == 1, targets, shapes[group]
            )
            order.leave(results[name][0])
        else:
            kept = stack_half(kept, come, mine).astype(F32)
            order.leave(kept)
            results.setdefault((layer, name), []).append(kept)

    def small_flow():
        gain = jnp.stack([acc[n][name] for name in ("gain1", "gain2") for n in range(LAYERS)])
        gain = lax.dynamic_update_slice_in_dim(jnp.zeros((2 * LAYERS, D), F32), gain, col_start, 1)
        bias = jnp.stack([acc[n]["bias"][:, :NEAR] for n in range(LAYERS)])
        bias = jnp.einsum("lhdc,dcb->lbh", bias, behind, precision=HIGH)
        bias = lax.dynamic_update_slice_in_dim(
            jnp.zeros((LAYERS, NB, H), F32), bias, head_start, 2
        )
        total = jnp.concatenate((gain.reshape(-1, 128), bias.reshape(-1, 128)), 0)
        for axis in ("gx", "gy", "dp"):
            (total,) = order.enter(total)
            total = axis_sum(total, axis)
            yield
            (total,) = order.enter(total)
            order.leave(total)
        split = gain.size // 128
        summed.append(total[:split].reshape(gain.shape))
        summed.append(total[split:].reshape(bias.shape))

    def weight_grads():
        for layer, name, left, right in later:
            last = name in acc[layer]
            have = acc[layer].get(name, (None, None))
            left = order.enter(*left)
            right = order.enter(*right)
            both = [dot(a, b, TN) for a in left for b in right]
            if last:
                both = [a + b for a, b in zip(have, both)]
            acc[layer][name] = both
            order.leave(both[1])
            if last:
                axis = 0 if name in ("down", "mix") else 1
                total = jnp.concatenate([item.astype(BF) for item in both], axis)
                order.leave(total)
                flow = batch_flow(layer, name, total, 0)
                next(flow)
                flows.append(flow)
        later.clear()

    def run_later():
        for flow in list(flows):
            if next(flow, "end") == "end":
                flows.remove(flow)
        weight_grads()

    def forward(micro):
        seg_all = segments[micro]
        row_segs = lax.dynamic_slice_in_dim(seg_all, block * row_count, row_count)
        keep = (row_segs != 0).astype(F32)[:, None]
        views = segment_views(seg_all)
        hidden = inputs[micro].astype(F32)
        saved = []
        for layer in range(LAYERS):
            w = layers[layer]
            scale1 = row_norm(hidden)
            normed = (hidden * scale1[:, None] * w["gain1"]).astype(BF)
            order.leave(normed)
            normed = token_gather(normed)
            yield
            (normed,) = order.enter(normed)
            come = core_swap(rows_dot([normed], w["qkv_half"][1:], NN))
            qkv = rows_dot([normed], w["qkv_half"][:1], NN, add_rounded, [come])
            own, lse = attend(qkv, *views, w["bias"])
            mixed = [own, core_swap(own)]
            branch = rows_dot(mixed, w["mix_half"], NN)
            order.leave(branch)
            branch = token_reduce(branch)
            yield
            (branch,) = order.enter(branch)
            middle = hidden + branch
            scale2 = row_norm(middle)
            dense = (middle * scale2[:, None] * w["gain2"]).astype(BF)
            order.leave(dense)
            dense = token_gather(dense)
            yield
            (dense,) = order.enter(dense)
            come = core_swap(rows_dot([dense], w["gu_half"][1:], NN))
            gate_up, active = rows_dot(
                [dense],
                w["gu_half"][:1],
                NN,
                gate_rounded,
                [come],
                (2 * hidden_dev, hidden_dev),
            )
            active = [active, core_swap(active)]
            out = rows_dot(active, w["down_half"], NN)
            order.leave(out)
            saved.append(
                (hidden, scale1, normed, qkv, lse, mixed, middle, scale2, dense)
                + (gate_up, active)
            )
            if layer == LAYERS - 1:
                break
            out = token_reduce(out)
            yield
            (out,) = order.enter(out)
            hidden = middle + out
        ends.append((middle, out, keep))
        grad = cotangent[micro].astype(F32) * keep
        for layer in reversed(range(LAYERS)):
            w = layers[layer]
            hidden, scale1, normed, qkv, lse, mixed = saved[layer][:6]
            middle, scale2, dense, gate_up, active = saved[layer][6:]
            grad_out = grad.astype(BF)
            order.leave(grad_out)
            grad_out = token_gather(grad_out)
            yield
            (grad_out,) = order.enter(grad_out)
            come = core_swap(rows_dot([grad_out], w["down_half"][1:], NT))
            pair = rows_dot(
                [grad_out],
                w["down_half"][:1],
                NT,
                gate_back_rounded,
                [come, gate_up],
                (2 * hidden_dev,),
            )
            pair = [pair, core_swap(pair)]
            grad_dense = rows_dot(pair, w["gu_half"], NT)
            order.leave(grad_dense)
            grad_dense = token_reduce(grad_dense)
            later.append((layer, "down", active, [grad_out]))
            later.append((layer, "gu", [dense], pair))
            yield
            (grad_dense,) = order.enter(grad_dense)
            grad_norm, gain_part = norm_back(grad_dense, middle, scale2, w["gain2"])
            add(layer, "gain2", gain_part)
            grad_mid = grad + grad_norm
            grad_out = grad_mid.astype(BF)
            order.leave(grad_out)
            grad_out = token_gather(grad_out)
            yield
            (grad_out,) = order.enter(grad_out)
            come = core_swap(rows_dot([grad_out], w["mix_half"][1:], NT))
            grad_mixed = rows_dot([grad_out], w["mix_half"][:1], NT, add_rounded, [come])
            if layer == 0 and micro == MICRO - 1:
                order.leave(grad_mixed)
                later.append((layer, "mix", mixed, [grad_out]))
                weight_grads()
                (grad_mixed,) = order.enter(grad_mixed)
            gq, gk, gv, gb = attend_back(qkv, *views, w["bias"], mixed[0], lse, grad_mixed)
            add(layer, "bias", gb)
            triple = jnp.concatenate((gq, gk, gv), 1)
            triple = [triple, core_swap(triple)]
            grad_normed = rows_dot(triple, w["qkv_half"], NT)
            order.leave(grad_normed)
            grad_normed = token_reduce(grad_normed)
            if layer == 0 and micro == MICRO - 1:
                for n, (middle, out, keep) in enumerate(ends):
                    (out,) = order.enter(out)
                    outputs[n] = (middle + token_reduce(out)) * keep
            if layer > 0 or micro < MICRO - 1:
                later.append((layer, "mix", mixed, [grad_out]))
            later.append((layer, "qkv", [normed], triple))
            yield
            (grad_normed,) = order.enter(grad_normed)
            grad_norm, gain_part = norm_back(grad_normed, hidden, scale1, w["gain1"])
            add(layer, "gain1", gain_part)
            grad = grad_mid + grad_norm
        grads[micro] = grad

    outputs = [None] * MICRO
    grads = [None] * MICRO
    micro_flows = [forward(micro) for micro in range(MICRO)]
    live = list(micro_flows)
    while live:
        for flow in list(live):
            if next(flow, "end") == "end":
                live.remove(flow)
        run_later()
    flow = small_flow()
    next(flow)
    flows.append(flow)
    while flows:
        run_later()
    gain, bias = summed
    if not tidy:
        for name, count in (("qkv", 3), ("gu", 2), ("mix", 1), ("down", 1)):
            axis = 0 if count == 1 else 1
            whole = []
            for layer in range(LAYERS):
                both = jnp.split(jnp.concatenate(results[layer, name], 0), 2, axis)
                ordered = in_order(*both, core, axis)
                whole.append([ordered] if count == 1 else unpaired(ordered, count))
            results[name] = [
                jnp.stack([whole[layer][n] for layer in range(LAYERS)]) for n in range(count)
            ]
    grad_query, grad_key, grad_value = results["qkv"]
    grad_gate, grad_up = results["gu"]
    (grad_mixing,) = results["mix"]
    (grad_down,) = results["down"]
    return (
        jnp.stack(outputs),
        jnp.stack(grads),
        gain[:LAYERS],
        grad_query,
        grad_key,
        grad_value,
        grad_mixing,
        bias,
        gain[LAYERS:],
        grad_gate,
        grad_up,
        grad_down,
    )


def solution(mesh):
    tokens = P(None, ("dp", "gy"), "gx")
    wide = P(None, "gx", "gy")
    tall = P(None, "gy", "gx")
    return jax.shard_map(
        body,
        mesh=mesh,
        in_specs=(tokens, tokens, P(None, "dp"), P())
        + (wide, wide, wide, tall, P(), P(), wide, wide, tall),
        out_specs=(tokens, tokens, P(), wide, wide, wide, tall, P(), P(), wide, wide, tall),
        check_vma=False,
    )
```

```python
import functools

import jax
import jax.numpy as jnp
from jax import lax
from jax.experimental import pallas as pl
from jax.experimental.pallas import tpu as pltpu
from jax.sharding import PartitionSpec as P

D = 2048
H = 32
DH = 64
NB = 32
LAYERS = 2
MICRO = 2
LEN = 1024
TILE = 256
NEAR = 5
NEG = -1000000000.0
HIGH = lax.Precision.HIGHEST
ROWS = 256
GELU_A = 0.7978845608028654
GELU_B = 0.044715


def lanes_of(head, heads):
    wide = min(2, heads) * DH
    start = head * DH // wide * wide
    return slice(start, start + wide)


def pick(values, head, heads):
    values = values[:, lanes_of(head, heads)]
    if heads == 1:
        return values
    lane = lax.broadcasted_iota(jnp.int32, values.shape, 1)
    return jnp.where((lane // DH) == head % 2, values, jnp.zeros_like(values))


def join(rows, heads):
    if heads == 1:
        return rows[0]
    return jnp.concatenate([rows[h][h % 2 * DH : h % 2 * DH + DH] for h in range(heads)], 0)


def nt(a, b):
    return lax.dot_general(a, b, (((1,), (1,)), ((), ())), preferred_element_type=jnp.float32)


def nn(a, b):
    return lax.dot_general(a, b, (((1,), (0,)), ((), ())), preferred_element_type=jnp.float32)


def build_bias(heads, w_ref, bias):
    for h in range(heads):
        for d in range(NEAR):
            wide = jnp.broadcast_to(w_ref[h, d : d + 1, :], (TILE, 2 * TILE))
            if 0 < d < NEAR - 1:
                wide = pltpu.roll(wide, 0, 1, stride=1, stride_axis=0)
            bias[h, d] = wide[:, :TILE]


def fwd_kernel(heads, span, segr, segc, q_ref, k_ref, v_ref, w_ref, o_ref, lse_ref, bias, turned):
    iq = pl.program_id(0)

    @pl.when(iq == 0)
    def _():
        build_bias(heads, w_ref, bias)
        turned[...] = v_ref[...].T

    q = q_ref[...]
    row_seg = segr[...]
    queries = [pick(q, h, heads) for h in range(heads)]
    wide = min(2, heads) * DH

    def step(kc, carry):
        rows = pl.ds(pl.multiple_of(kc * TILE, TILE), TILE)
        near = jnp.clip(kc - iq + 2, 0, NEAR - 1)
        allowed = segc[rows, :] == row_seg
        k = k_ref[rows, :]
        out = []
        for h in range(heads):
            high, total, acc = carry[h]
            s = nt(k[:, lanes_of(h, heads)], queries[h]) + bias[h, near]
            s = jnp.where(allowed, s, NEG)
            top = jnp.maximum(high, jnp.max(s, axis=0, keepdims=True))
            scale = jnp.exp(high - top)
            e = jnp.exp(s - top)
            total = total * scale + jnp.sum(e, axis=0, keepdims=True)
            acc = acc * scale + nn(turned[lanes_of(h, heads), rows], e.astype(jnp.bfloat16))
            out.append((top, total, acc))
        return tuple(out)

    start = (
        jnp.full((1, TILE), 2 * NEG, jnp.float32),
        jnp.zeros((1, TILE), jnp.float32),
        jnp.zeros((wide, TILE), jnp.float32),
    )
    done = lax.fori_loop(span[0, iq], span[1, iq], step, (start,) * heads)
    lse_ref[...] = jnp.zeros_like(lse_ref)
    for h in range(heads):
        lse_ref[h : h + 1, :] = done[h][0] + jnp.log(done[h][1])
    out = join([acc / total for _, total, acc in done], heads)
    o_ref[...] = out.T.astype(o_ref.dtype)


def bwd_kernel(
    heads,
    span,
    segr,
    segc,
    q_ref,
    k_ref,
    v_ref,
    w_ref,
    o_ref,
    lse_ref,
    go_ref,
    gq_ref,
    gk_ref,
    gv_ref,
    gb_ref,
    bias,
    gbias,
    gk_acc,
    gv_acc,
    turned,
):
    iq = pl.program_id(0)

    @pl.when(iq == 0)
    def _():
        build_bias(heads, w_ref, bias)
        turned[...] = k_ref[...].T
        gbias[...] = jnp.zeros_like(gbias)
        gk_acc[...] = jnp.zeros_like(gk_acc)
        gv_acc[...] = jnp.zeros_like(gv_acc)

    q = q_ref[...]
    go = go_ref[...]
    row_seg = segr[...]
    prod = (o_ref[...].astype(jnp.float32) * go.astype(jnp.float32)).T
    queries = [pick(q, h, heads) for h in range(heads)]
    outs = [pick(go, h, heads) for h in range(heads)]
    lse = [lse_ref[h : h + 1, :] for h in range(heads)]
    delta = [
        jnp.sum(prod[h * DH : (h + 1) * DH, :], axis=0, keepdims=True) for h in range(heads)
    ]
    wide = min(2, heads) * DH

    def step(kc, carry):
        rows = pl.ds(pl.multiple_of(kc * TILE, TILE), TILE)
        near = jnp.clip(kc - iq + 2, 0, NEAR - 1)
        allowed = segc[rows, :] == row_seg
        k = k_ref[rows, :]
        v = v_ref[rows, :]
        result = []
        for h in range(heads):
            lanes = lanes_of(h, heads)
            s = nt(k[:, lanes], queries[h]) + bias[h, near]
            s = jnp.where(allowed, s, NEG)
            p = jnp.exp(s - lse[h])
            gp = nt(v[:, lanes], outs[h])
            gs = (p * (gp - delta[h])).astype(jnp.bfloat16)
            gv_acc[rows, lanes] += nn(p.astype(jnp.bfloat16), outs[h])
            gk_acc[rows, lanes] += nn(gs, queries[h])
            gbias[h, near] += gs.astype(jnp.float32)
            result.append(carry[h] + nn(turned[lanes, rows], gs))
        return tuple(result)

    start = (jnp.zeros((wide, TILE), jnp.float32),) * heads
    done = lax.fori_loop(span[0, iq], span[1, iq], step, start)
    gq_ref[...] = join(done, heads).T.astype(gq_ref.dtype)

    @pl.when(iq == pl.num_programs(0) - 1)
    def _():
        gk_ref[...] = gk_acc[...].astype(gk_ref.dtype)
        gv_ref[...] = gv_acc[...].astype(gv_ref.dtype)
        gb_ref[...] = jnp.zeros_like(gb_ref)
        down = lax.broadcasted_iota(jnp.int32, (TILE, TILE), 0)
        across = lax.broadcasted_iota(jnp.int32, (TILE, TILE), 1)
        flip = (down + across == TILE - 1).astype(jnp.float32)
        for h in range(heads):
            for d in range(NEAR):
                tile = gbias[h, d]
                if 0 < d < NEAR - 1:
                    tile = lax.dot_general(
                        flip,
                        tile,
                        (((1,), (0,)), ((), ())),
                        precision=HIGH,
                        preferred_element_type=jnp.float32,
                    )
                wide = jnp.concatenate([tile, jnp.zeros_like(tile)], axis=1)
                if 0 < d < NEAR - 1:
                    wide = pltpu.roll(wide, 0, 1, stride=1, stride_axis=0)
                gb_ref[h, d : d + 1, :] = jnp.sum(wide, axis=0, keepdims=True)


def parts_of(qkv, width):
    if width % 128 == 0:
        return [(qkv, n) for n in range(3)]
    return [(qkv[:, n * width : (n + 1) * width], 0) for n in range(3)]


def seen_specs(qkv, heads):
    width = heads * DH
    (qa, q0), (ka, k0), (va, v0) = parts_of(qkv, width)
    specs = [
        pl.BlockSpec((1, TILE), lambda i, s: (0, i)),
        pl.BlockSpec((LEN, 1), lambda i, s: (0, 0)),
        pl.BlockSpec((TILE, width), lambda i, s: (i, q0)),
        pl.BlockSpec((LEN, width), lambda i, s: (0, k0)),
        pl.BlockSpec((LEN, width), lambda i, s: (0, v0)),
        pl.BlockSpec((heads, NEAR, 2 * TILE), lambda i, s: (0, 0, 0)),
    ]
    return specs, (qa, ka, va)


def attend(qkv, span, segr, segc, w):
    heads = w.shape[0]
    width = heads * DH
    specs, parts = seen_specs(qkv, heads)
    tile = pl.BlockSpec((TILE, width), lambda i, s: (i, 0))
    sums = pl.BlockSpec((8, TILE), lambda i, s: (0, i))
    grid = pltpu.PrefetchScalarGridSpec(
        num_scalar_prefetch=1,
        grid=(LEN // TILE,),
        in_specs=specs,
        out_specs=[tile, sums],
        scratch_shapes=[
            pltpu.VMEM((heads, NEAR, TILE, TILE), jnp.float32),
            pltpu.VMEM((width, LEN), jnp.bfloat16),
        ],
    )
    return pl.pallas_call(
        functools.partial(fwd_kernel, heads),
        grid_spec=grid,
        out_shape=[
            jax.ShapeDtypeStruct((LEN, width), jnp.bfloat16),
            jax.ShapeDtypeStruct((8, LEN), jnp.float32),
        ],
        compiler_params=pltpu.CompilerParams(vmem_limit_bytes=40 * 1024 * 1024),
        cost_estimate=pl.CostEstimate(flops=0, bytes_accessed=0, transcendentals=0),
    )(span, segr, segc, *parts, w)


def bwd_waiting(heads, waits, *refs):
    bwd_kernel(heads, *refs[:10], *refs[10 + waits :])


def attend_back(qkv, span, segr, segc, w, o, lse, go, after):
    heads = w.shape[0]
    width = heads * DH
    specs, parts = seen_specs(qkv, heads)
    tile = pl.BlockSpec((TILE, width), lambda i, s: (i, 0))
    sums = pl.BlockSpec((8, TILE), lambda i, s: (0, i))
    whole = pl.BlockSpec((LEN, width), lambda i, s: (0, 0))
    grid = pltpu.PrefetchScalarGridSpec(
        num_scalar_prefetch=1,
        grid=(LEN // TILE,),
        in_specs=specs + [tile, sums, tile] + [pl.BlockSpec(memory_space=pl.ANY)] * len(after),
        out_specs=[tile, whole, whole, pl.BlockSpec((heads, 8, 2 * TILE), lambda i, s: (0, 0, 0))],
        scratch_shapes=[pltpu.VMEM((heads, NEAR, TILE, TILE), jnp.float32)] * 2
        + [pltpu.VMEM((LEN, width), jnp.float32)] * 2
        + [pltpu.VMEM((width, LEN), jnp.bfloat16)],
    )
    flat = jax.ShapeDtypeStruct((LEN, width), jnp.bfloat16)
    return pl.pallas_call(
        functools.partial(bwd_waiting, heads, len(after)),
        grid_spec=grid,
        out_shape=[flat, flat, flat, jax.ShapeDtypeStruct((heads, 8, 2 * TILE), jnp.float32)],
        compiler_params=pltpu.CompilerParams(vmem_limit_bytes=40 * 1024 * 1024),
        cost_estimate=pl.CostEstimate(flops=0, bytes_accessed=0, transcendentals=0),
    )(span, segr, segc, *parts, w, o, lse, go, *after)


THRESHOLDS = (12, 16, 23, 32, 46, 64, 91)
def bucket_of(offset):
    distance = jnp.abs(offset)
    beyond = 8 + sum(((distance >= threshold).astype(jnp.int32) for threshold in THRESHOLDS))
    within = jnp.where(distance < 8, distance, beyond)
    return jnp.where(offset > 0, 16, 0) + within

def near_table(back):
    place = jnp.arange(2*TILE, dtype=jnp.int32)
    turn = place - (TILE - 1) if back else jnp.where(place < TILE, place, place - 2*TILE)
    offset = TILE*(jnp.arange(NEAR, dtype=jnp.int32) - 2)[:, None] - turn[None, :]
    return (bucket_of(offset)[:, :, None] == jnp.arange(NB, dtype=jnp.int32)).astype(jnp.float32)

def segment_views(segment):
    places = jnp.arange(LEN, dtype=jnp.int32)
    own = jnp.where(segment == 0, 4 + places, segment)
    order = jnp.where(segment == 0, 4, segment).reshape(-1, TILE)
    low, high = order[:, 0], order[:, -1]
    lo = jnp.sum((high[None, :] < low[:, None]).astype(jnp.int32), axis=1)
    hi = jnp.sum((low[None, :] <= high[:, None]).astype(jnp.int32), axis=1)
    return jnp.stack((lo, hi)), own[None, :], own[:, None]


NN = ((1,), (0,))
NT = ((1,), (1,))
TN = ((0,), (0,))
BF = jnp.bfloat16
F32 = jnp.float32


def core_swap(values):
    return lax.ppermute(values, "gx", [(0, 1), (1, 0)])


def token_gather(values):
    return lax.all_gather(values, "gy", axis=0, tiled=True)


def token_reduce(values):
    return lax.psum_scatter(values, "gy", scatter_dimension=0, tiled=True).astype(F32)


def shifted(values, step):
    size = lax.axis_size("gy")
    return lax.ppermute(values, "gy", [(n, (n + step) % size) for n in range(size)])


def dot(left, right, dims):
    return lax.dot_general(left, right, (dims, ((), ())), preferred_element_type=F32)


def rows_kernel(dims, count, extras, waits, finish, *refs):
    total = None
    for n in range(count):
        part = dot(refs[n][...], refs[count + n][...], dims)
        total = part if total is None else total + part
    inner = 2 * count + extras
    finish(total, [ref[...] for ref in refs[2 * count : inner]], refs[inner + waits :])


def keep_rounded(total, extras, outs):
    outs[0][...] = total.astype(BF)


def add_rounded(total, extras, outs):
    outs[0][...] = (total + extras[0].astype(F32)).astype(BF)


def gelu_parts(gate):
    inner = GELU_A * (gate + GELU_B * gate * gate * gate)
    half = 0.5 * (1.0 + jnp.tanh(inner))
    return half, gate * half


def gate_rounded(total, extras, outs):
    total = total + extras[0].astype(F32)
    width = total.shape[1] // 2
    gate, up = total[:, :width], total[:, width:]
    outs[0][...] = total.astype(BF)
    outs[1][...] = (gelu_parts(gate)[1] * up).astype(BF)


def gate_back_rounded(total, extras, outs):
    grad = total + extras[0].astype(F32)
    width = grad.shape[1]
    gate = extras[1][:, :width].astype(F32)
    up = extras[1][:, width:].astype(F32)
    half, value = gelu_parts(gate)
    slope = half + 2.0 * gate * half * (1.0 - half) * GELU_A * (1.0 + 3.0 * GELU_B * gate * gate)
    outs[0][:, :width] = (grad * up * slope).astype(BF)
    outs[0][:, width:] = (grad * value).astype(BF)


def rows_dot(parts, weights, dims, finish=keep_rounded, extras=(), widths=None, after=()):
    rows = parts[0].shape[0]
    if widths is None:
        widths = (weights[0].shape[1 - dims[1][0]],)
    outs = [jax.ShapeDtypeStruct((rows, width), BF) for width in widths]
    if not all(item.shape[1] % 128 == 0 for item in (*parts, *weights, *extras, *outs)):
        return plain_dot(parts, weights, dims, finish, extras, outs)
    tall = min(rows, ROWS)

    def sliced(item):
        return pl.BlockSpec((tall, item.shape[1]), lambda i: (i, 0))

    def whole(item):
        return pl.BlockSpec(item.shape, lambda i: (0, 0))

    result = pl.pallas_call(
        functools.partial(rows_kernel, dims, len(parts), len(extras), len(after), finish),
        grid=(rows // tall,),
        in_specs=[sliced(item) for item in parts]
        + [whole(item) for item in weights]
        + [sliced(item) for item in extras]
        + [pl.BlockSpec(memory_space=pl.ANY)] * len(after),
        out_specs=[sliced(item) for item in outs],
        out_shape=outs,
        compiler_params=pltpu.CompilerParams(vmem_limit_bytes=40 * 1024 * 1024),
        cost_estimate=pl.CostEstimate(flops=0, bytes_accessed=0, transcendentals=0),
    )(*parts, *weights, *extras, *after)
    return result[0] if len(outs) == 1 else result


def join_kernel(count, waits, *refs):
    width = refs[0].shape[1]
    for n in range(count):
        refs[count + waits][:, n * width : (n + 1) * width] = refs[n][...]


def rows_join(parts, after):
    rows, width = parts[0].shape
    count = len(parts)
    if width % 128:
        return jnp.concatenate(parts, 1)
    tall = min(rows, ROWS)
    return pl.pallas_call(
        functools.partial(join_kernel, count, len(after)),
        grid=(rows // tall,),
        in_specs=[pl.BlockSpec((tall, width), lambda i: (i, 0))] * count
        + [pl.BlockSpec(memory_space=pl.ANY)] * len(after),
        out_specs=pl.BlockSpec((tall, count * width), lambda i: (i, 0)),
        out_shape=jax.ShapeDtypeStruct((rows, count * width), BF),
        compiler_params=pltpu.CompilerParams(vmem_limit_bytes=40 * 1024 * 1024),
        cost_estimate=pl.CostEstimate(flops=0, bytes_accessed=0, transcendentals=0),
    )(*parts, *after)


def grads_kernel(groups, micros, waits, blocks, mine, *refs):
    kept, sent = refs[-2:]
    ours = (pl.program_id(0) // blocks) == mine[0]
    rights = sum(groups)
    each = len(groups) + rights
    column = 0
    for g, size in enumerate(groups):
        turned = [refs[n * each + g][...].T for n in range(micros)]
        first = len(groups) + sum(groups[:g])
        for j in range(first, first + size):
            total = sum(dot(turned[n], refs[n * each + j][...], NN) for n in range(micros))
            total = total.astype(BF)
            place = slice(column, column + total.shape[1])
            column = place.stop

            @pl.when(ours)
            def _():
                kept[:, place] = total

            @pl.when(jnp.logical_not(ours))
            def _():
                sent[:, place] = total


def half_spec(rows, width, blocks, ours):
    def index(i, s):
        which = s[0] if ours else 1 - s[0]
        return jnp.clip(i - which * blocks, 0, blocks - 1), 0

    return pl.BlockSpec((rows, width), index)


def local_call(kernel, scalar, grid, in_specs, out_specs, out_shape, arrays, after):
    spec = pltpu.PrefetchScalarGridSpec(
        num_scalar_prefetch=1,
        grid=grid,
        in_specs=in_specs + [pl.BlockSpec(memory_space=pl.ANY)] * len(after),
        out_specs=out_specs,
    )
    return pl.pallas_call(
        kernel,
        grid_spec=spec,
        out_shape=out_shape,
        compiler_params=pltpu.CompilerParams(vmem_limit_bytes=56 * 1024 * 1024),
        cost_estimate=pl.CostEstimate(flops=0, bytes_accessed=0, transcendentals=0),
    )(scalar.astype(jnp.int32).reshape(1), *arrays, *after)


def packed_grads(items, mine, after):
    groups = [len(rights) for _, rights in items[0]]
    depth = items[0][0][0].shape[1]
    if any(right.shape[1] % 128 for _, rights in items[0] for right in rights):
        result = []
        for g, size in enumerate(groups):
            for j in range(size):
                parts = [dot(item[g][0], item[g][1][j], TN) for item in items]
                result.append(sum(parts).astype(BF))
        total = jnp.concatenate(result, 1)
        return take_half(total, mine), take_half(total, 1 - mine)
    arrays, specs = [], []
    for item in items:
        for left, _ in item:
            arrays.append(left)
            specs.append(pl.BlockSpec((left.shape[0], ROWS), lambda i, s: (0, i)))
        for _, rights in item:
            arrays.extend(rights)
            specs.extend(pl.BlockSpec(right.shape, lambda i, s: (0, 0)) for right in rights)
    width = sum(right.shape[1] for _, rights in items[0] for right in rights)
    blocks = depth // ROWS // 2
    return local_call(
        functools.partial(grads_kernel, groups, len(items), len(after), blocks),
        mine,
        (2 * blocks,),
        specs,
        [half_spec(ROWS, width, blocks, ours) for ours in (True, False)],
        [jax.ShapeDtypeStruct((depth // 2, width), BF)] * 2,
        arrays,
        after,
    )


def halve_kernel(waits, blocks, mine, have, come, *refs):
    kept, sent = refs[waits:]
    total = (have[...].astype(F32) + come[...].astype(F32)).astype(BF)
    ours = (pl.program_id(0) // blocks) == mine[0]

    @pl.when(ours)
    def _():
        kept[...] = total

    @pl.when(jnp.logical_not(ours))
    def _():
        sent[...] = total


def halve(have, come, mine, after):
    rows, width = have.shape
    if width % 128 or rows % 64:
        total = (have.astype(F32) + come.astype(F32)).astype(BF)
        return take_half(total, mine), take_half(total, 1 - mine)
    tall = rows // 4
    return local_call(
        functools.partial(halve_kernel, len(after), 2),
        mine,
        (4,),
        [pl.BlockSpec((tall, width), lambda i, s: (i, 0))] * 2,
        [half_spec(tall, width, 2, ours) for ours in (True, False)],
        [jax.ShapeDtypeStruct((rows // 2, width), BF)] * 2,
        [have, come],
        after,
    )


def total_kernel(waits, mine, have, come, *refs):
    refs[waits][...] = (have[...].astype(F32) + come[...].astype(F32)).astype(BF)


def double_kernel(waits, blocks, mine, own, come, *refs):
    ours = (pl.program_id(0) // blocks) == mine[0]

    @pl.when(ours)
    def _():
        refs[waits][...] = own[...]

    @pl.when(jnp.logical_not(ours))
    def _():
        refs[waits][...] = come[...]


def arrive_kernel(*refs):
    refs[-1][...] = jnp.zeros_like(refs[-1])


def arrived(come, after):
    return pl.pallas_call(
        arrive_kernel,
        in_specs=[pl.BlockSpec(memory_space=pl.ANY)] * (1 + len(after)),
        out_shape=jax.ShapeDtypeStruct((8, 128), F32),
        cost_estimate=pl.CostEstimate(flops=0, bytes_accessed=0, transcendentals=0),
    )(come, *after)


def total_of(have, come, mine, after):
    rows, width = have.shape
    if width % 128 or rows % 32:
        return (have.astype(F32) + come.astype(F32)).astype(BF)
    tall = rows // 2
    spec = pl.BlockSpec((tall, width), lambda i, s: (i, 0))
    shape = jax.ShapeDtypeStruct((rows, width), BF)
    kernel = functools.partial(total_kernel, len(after))
    return local_call(kernel, mine, (2,), [spec] * 2, spec, shape, [have, come], after)


def double(own, come, mine, after):
    rows, width = own.shape
    if width % 128 or rows % 32:
        return stack_half(own, come, mine)
    tall = rows // 2
    return local_call(
        functools.partial(double_kernel, len(after), 2),
        mine,
        (4,),
        [half_spec(tall, width, 2, ours) for ours in (True, False)],
        pl.BlockSpec((tall, width), lambda i, s: (i, 0)),
        jax.ShapeDtypeStruct((2 * rows, width), BF),
        [own, come],
        after,
    )


class Holder:
    def __init__(self, shape):
        self.value = jnp.zeros(shape.shape, shape.dtype)

    def __setitem__(self, place, value):
        self.value = value if place is Ellipsis else self.value.at[place].set(value)


def plain_dot(parts, weights, dims, finish, extras, outs):
    total = sum(dot(part, weight, dims) for part, weight in zip(parts, weights))
    held = [Holder(item) for item in outs]
    finish(total, extras, held)
    return held[0].value if len(held) == 1 else [item.value for item in held]


def row_norm(hidden):
    part = jnp.sum(hidden * hidden, axis=1)
    return lax.rsqrt((part + core_swap(part)) / D + 1e-06)


def norm_back(grad_norm, hidden, scale, gain):
    weighted = grad_norm * gain
    part = jnp.sum(weighted * hidden, axis=1)
    inner = part + core_swap(part)
    cubed = scale * scale * scale * inner / D
    grad_hidden = scale[:, None] * weighted - hidden * cubed[:, None]
    gain_grad = jnp.sum(grad_norm * hidden * scale[:, None], axis=0)
    return grad_hidden, gain_grad


def halves(weights, axis, core):
    width = weights.shape[axis] // 2
    own = lax.dynamic_slice_in_dim(weights, core * width, width, axis)
    other = lax.dynamic_slice_in_dim(weights, (1 - core) * width, width, axis)
    return own, other


def in_order(own, other, core, axis):
    return jnp.where(
        core == 0,
        jnp.concatenate((own, other), axis),
        jnp.concatenate((other, own), axis),
    )


def paired(*weights):
    cut = [jnp.split(item, 2, axis=1) for item in weights]
    return jnp.concatenate([item[n] for n in range(2) for item in cut], 1)


def link_swap(values, bits):
    size = lax.axis_size("dp")
    pairs = [(n * 2 + c, (n ^ bits[c]) * 2 + c) for n in range(size) for c in range(2)]
    return lax.ppermute(values, ("dp", "gx"), pairs)


def take_half(values, which):
    rows = values.shape[0] // 2
    return lax.dynamic_slice_in_dim(values, which * rows, rows, 0)


def stack_half(own, other, which):
    return jnp.where(
        which == 0,
        jnp.concatenate((own, other), 0),
        jnp.concatenate((other, own), 0),
    )


def batch_steps(place, core):
    size = lax.axis_size("dp")
    bits = [1 << n for n in range(size.bit_length() - 1)]
    steps = []
    for first, second in zip(bits, bits[::-1]):
        bit = jnp.where(core == 0, first, second)
        steps.append(((first, second), jnp.where((place & bit) != 0, 1, 0)))
    return steps


def settle_kernel(count, waits, blocks, place, own_ref, other_ref, *refs):
    outs = refs[waits:]
    half = pl.program_id(0) // blocks

    def store(values, core):
        width = outs[0].shape[2] // 2
        tall = outs[count].shape[1] // 2
        for part in range(2):
            spot = part ^ core
            for n in range(count):
                start = (part * count + n) * width
                cut = values[:, start : start + width].astype(F32)
                outs[n][0, :, spot * width : (spot + 1) * width] = cut
            start = 2 * count * width + part * tall
            cut = values[:, start : start + tall].astype(F32)
            outs[count][0, spot * tall : (spot + 1) * tall, :] = cut.T

    for source, ref in enumerate((own_ref, other_ref)):
        for core in range(2):

            @pl.when(((half ^ place[0]) == source) & (place[1] == core))
            def _():
                store(ref[...], core)


def settle(own, other, flag, core, layer, targets, shapes, after):
    rows = 128
    blocks = own.shape[0] // rows

    def block(source):
        def index(i, s):
            return jnp.where(((i // blocks) ^ s[0]) == source, i % blocks, 0), 0

        return pl.BlockSpec((rows, own.shape[1]), index)

    count = len(shapes) - 1
    grid = pltpu.PrefetchScalarGridSpec(
        num_scalar_prefetch=1,
        grid=(2 * blocks,),
        in_specs=[block(0), block(1)]
        + [pl.BlockSpec(memory_space=pl.ANY)] * (len(targets) + len(after)),
        out_specs=[
            pl.BlockSpec((1, rows, item.shape[2]), lambda i, s: (layer, i, 0))
            for item in shapes[:count]
        ]
        + [pl.BlockSpec((1, shapes[count].shape[1], rows), lambda i, s: (layer, 0, i))],
    )
    return pl.pallas_call(
        functools.partial(settle_kernel, count, len(targets) + len(after), blocks),
        grid_spec=grid,
        out_shape=shapes,
        input_output_aliases={3 + n: n for n in range(len(targets))},
        compiler_params=pltpu.CompilerParams(vmem_limit_bytes=40 * 1024 * 1024),
        cost_estimate=pl.CostEstimate(flops=0, bytes_accessed=0, transcendentals=0),
    )(jnp.stack((flag, core)).astype(jnp.int32), own, other, *targets, *after)


def plain_settle(values, core, shapes):
    count = len(shapes) - 1
    width = shapes[0].shape[2] // 2
    cut = [values[:, n * width : (n + 1) * width] for n in range(2 * count)]
    done = [in_order(cut[n], cut[count + n], core, 1) for n in range(count)]
    own, other = jnp.split(values[:, 2 * count * width :].T, 2, 0)
    return done + [in_order(own, other, core, 0)]


def axis_sum(values, axis):
    size = lax.axis_size(axis)

    def swapped(item, bits):
        return lax.ppermute(item, axis, [(n, n ^ bits) for n in range(size)])

    if size == 4:
        one, two, three = (swapped(values, bits) for bits in (1, 2, 3))
        return (values + one) + (two + three)
    bit = 1
    while bit < size:
        values = values + swapped(values, bit)
        bit *= 2
    return values


GROUPS = ("ffn", "attn")


class Order:
    def __init__(self):
        self.last = None
        self.dues = []
        self.slow = []
        self.gate = []

    def enter(self, *values):
        if self.last is None:
            return values
        return lax.optimization_barrier((*values, self.last))[:-1]

    def leave(self, value):
        self.last = value

    def due(self, value):
        self.dues.append(value)

    def take(self):
        dues, self.dues = self.dues, []
        return dues

    def take_slow(self):
        dues, self.slow = self.slow, []
        return dues


def body(
    inputs,
    cotangent,
    segments,
    attention_gain,
    query_weight,
    key_weight,
    value_weight,
    mixing_weight,
    relative_bias,
    dense_gain,
    gate_weight,
    up_weight,
    down_weight,
):
    core = lax.axis_index("gx")
    block = lax.axis_index("gy")
    place = lax.axis_index("dp")
    row_count = inputs.shape[1]
    col_count = inputs.shape[2]
    col_start = core * col_count
    heads_dev = query_weight.shape[2] // (2 * DH)
    head_start = (block * 2 + core) * heads_dev
    hidden_dev = gate_weight.shape[2] // 2
    ahead = near_table(False)
    behind = near_table(True)
    steps = batch_steps(place, core)
    order = Order()
    later = {}
    flows = {}
    summed = []
    ends = []
    results = {}
    tidy = hidden_dev % 128 == 0 and (heads_dev * DH) % 128 == 0
    shapes = {
        kind: [jax.ShapeDtypeStruct(item.shape, F32) for item in group]
        for kind, group in (
            ("attn", (query_weight, key_weight, value_weight, mixing_weight)),
            ("ffn", (gate_weight, up_weight, down_weight)),
        )
    }
    layers = []
    for layer in range(LAYERS):
        qkv = paired(query_weight[layer], key_weight[layer], value_weight[layer])
        gu = paired(gate_weight[layer], up_weight[layer])
        table = lax.dynamic_slice_in_dim(relative_bias[layer], head_start, heads_dev, 1)
        layers.append(
            dict(
                qkv_half=halves(qkv, 1, core),
                gu_half=halves(gu, 1, core),
                mix_half=halves(mixing_weight[layer], 0, core),
                down_half=halves(down_weight[layer], 0, core),
                bias=jnp.einsum("dcb,bh->hdc", ahead, table, precision=HIGH),
                gain1=lax.dynamic_slice_in_dim(attention_gain[layer], col_start, col_count),
                gain2=lax.dynamic_slice_in_dim(dense_gain[layer], col_start, col_count),
            )
        )
    acc = [dict() for _ in range(LAYERS)]

    def add(layer, name, value):
        have = acc[layer].get(name)
        acc[layer][name] = value if have is None else have + value

    def batch_flow(layer, kind, kept, sent):
        (bits1, mine1), (bits2, mine2) = steps
        come = link_swap(sent, bits1)
        yield
        kept, sent = halve(kept, come, mine2, order.gate)
        order.due(kept)
        come = link_swap(sent, bits2)
        yield
        kept = total_of(kept, come, mine2, order.gate)
        order.due(kept)
        come = link_swap(kept, bits2)
        yield
        kept = double(kept, come, mine2, order.gate)
        order.due(kept)
        come = link_swap(kept, bits1)
        yield
        order.due(arrived(come, order.gate))
        yield
        if tidy:
            targets = results.get(kind, [])
            results[kind] = settle(
                kept, come, mine1, core, layer, targets, shapes[kind], order.gate
            )
            order.slow.append(results[kind][0])
        else:
            kept = stack_half(kept, come, mine1).astype(F32)
            results[layer, kind] = plain_settle(kept, core, shapes[kind])

    def small_flow():
        gain = jnp.stack([acc[n][name] for name in ("gain1", "gain2") for n in range(LAYERS)])
        gain = lax.dynamic_update_slice_in_dim(jnp.zeros((2 * LAYERS, D), F32), gain, col_start, 1)
        bias = jnp.stack([acc[n]["bias"][:, :NEAR] for n in range(LAYERS)])
        bias = jnp.einsum("lhdc,dcb->lbh", bias, behind, precision=HIGH)
        bias = lax.dynamic_update_slice_in_dim(
            jnp.zeros((LAYERS, NB, H), F32), bias, head_start, 2
        )
        total = jnp.concatenate((gain.reshape(-1, 128), bias.reshape(-1, 128)), 0)
        for axis in ("gx", "gy", "dp"):
            total = axis_sum(total, axis)
            yield
        split = gain.size // 128
        summed.append(total[:split].reshape(gain.shape))
        summed.append(total[split:].reshape(bias.shape))

    def weight_grads():
        for (layer, kind), items in list(later.items()):
            if len(items) == MICRO:
                before = order.last
                if kind == "ffn":
                    advance("attn", layer + 1)
                kept, sent = packed_grads(items, steps[0][1], [before, *order.take()])
                order.leave(kept)
                flow = batch_flow(layer, kind, kept, sent)
                next(flow)
                flows[kind, layer] = flow
                del later[layer, kind]

    def advance(kind, layer, gate=None):
        order.gate = [order.last if gate is None else gate]
        if (kind, layer) in flows and next(flows[kind, layer], "end") == "end":
            del flows[kind, layer]

    def forward(micro):
        seg_all = segments[micro]
        row_segs = lax.dynamic_slice_in_dim(seg_all, block * row_count, row_count)
        keep = (row_segs != 0).astype(F32)[:, None]
        views = segment_views(seg_all)
        hidden = inputs[micro].astype(F32)
        saved = []
        for layer in range(LAYERS):
            w = layers[layer]
            scale1 = row_norm(hidden)
            normed = (hidden * scale1[:, None] * w["gain1"]).astype(BF)
            order.leave(normed)
            normed = token_gather(normed)
            yield
            (normed,) = order.enter(normed)
            come = core_swap(rows_dot([normed], w["qkv_half"][1:], NN))
            qkv = rows_dot([normed], w["qkv_half"][:1], NN, add_rounded, [come])
            own, lse = attend(qkv, *views, w["bias"])
            mixed = [own, core_swap(own)]
            branch = rows_dot(mixed, w["mix_half"], NN)
            order.leave(branch)
            branch = token_reduce(branch)
            yield
            (branch,) = order.enter(branch)
            middle = hidden + branch
            scale2 = row_norm(middle)
            dense = (middle * scale2[:, None] * w["gain2"]).astype(BF)
            order.leave(dense)
            dense = token_gather(dense)
            yield
            (dense,) = order.enter(dense)
            come = core_swap(rows_dot([dense], w["gu_half"][1:], NN))
            gate_up, active = rows_dot(
                [dense],
                w["gu_half"][:1],
                NN,
                gate_rounded,
                [come],
                (2 * hidden_dev, hidden_dev),
            )
            active = [active, core_swap(active)]
            saved.append(
                (hidden, scale1, normed, qkv, lse, mixed, middle, scale2, dense)
                + (gate_up, active)
            )
            if layer == LAYERS - 1:
                break
            out = rows_dot(active, w["down_half"], NN)
            order.leave(out)
            out = token_reduce(out)
            yield
            (out,) = order.enter(out)
            hidden = middle + out
        ends.append((middle, active, w["down_half"], keep))
        grad = cotangent[micro].astype(F32) * keep
        for layer in reversed(range(LAYERS)):
            w = layers[layer]
            hidden, scale1, normed, qkv, lse, mixed = saved[layer][:6]
            middle, scale2, dense, gate_up, active = saved[layer][6:]
            grad_out = grad.astype(BF)
            order.leave(grad_out)
            grad_out = token_gather(grad_out)
            yield
            (grad_out,) = order.enter(grad_out)
            if micro == 0:
                advance("ffn", layer + 1)
            advance("attn", layer + 1)
            dues = order.take()
            come = core_swap(rows_dot([grad_out], w["down_half"][1:], NT, after=dues))
            pair = rows_dot(
                [grad_out],
                w["down_half"][:1],
                NT,
                gate_back_rounded,
                [come, gate_up],
                (2 * hidden_dev,),
            )
            pair = [pair, core_swap(pair)]
            grad_dense = rows_dot(pair, w["gu_half"], NT, after=order.take())
            order.leave(grad_dense)
            grad_dense = token_reduce(grad_dense)
            item = [(dense, pair), (grad_out, active)]
            later.setdefault((layer, "ffn"), []).append(item)
            yield
            (grad_dense,) = order.enter(grad_dense)
            grad_norm, gain_part = norm_back(grad_dense, middle, scale2, w["gain2"])
            add(layer, "gain2", gain_part)
            grad_mid = grad + grad_norm
            grad_out = grad_mid.astype(BF)
            order.leave(grad_out)
            grad_out = token_gather(grad_out)
            yield
            (grad_out,) = order.enter(grad_out)
            if micro == 0:
                advance("ffn", layer)
            dues = order.take()
            come = core_swap(rows_dot([grad_out], w["mix_half"][1:], NT, after=dues))
            grad_mixed = rows_dot([grad_out], w["mix_half"][:1], NT, add_rounded, [come])
            gq, gk, gv, gb = attend_back(
                qkv, *views, w["bias"], mixed[0], lse, grad_mixed, order.take()
            )
            add(layer, "bias", gb)
            advance("ffn", layer, gq)
            triple = rows_join((gq, gk, gv), order.take())
            triple = [triple, core_swap(triple)]
            grad_normed = rows_dot(triple, w["qkv_half"], NT)
            order.leave(grad_normed)
            grad_normed = token_reduce(grad_normed)
            item = [(normed, triple), (grad_out, mixed)]
            later.setdefault((layer, "attn"), []).append(item)
            yield
            (grad_normed,) = order.enter(grad_normed)
            grad_norm, gain_part = norm_back(grad_normed, hidden, scale1, w["gain1"])
            add(layer, "gain1", gain_part)
            grad = grad_mid + grad_norm
        grads[micro] = grad

    outputs = [None] * MICRO
    grads = [None] * MICRO
    micro_flows = [forward(micro) for micro in range(MICRO)]
    live = list(micro_flows)
    while live:
        for flow in list(live):
            if next(flow, "end") == "end":
                live.remove(flow)
        weight_grads()
    advance("ffn", 0)
    after = [order.last, *order.take()]
    last = [rows_dot(active, down, NN, after=after) for _, active, down, _ in ends]
    after = last[-1]
    last = jnp.split(token_reduce(jnp.concatenate(last, 1)), MICRO, 1)
    for n, (middle, _, _, keep) in enumerate(ends):
        outputs[n] = (middle + last[n]) * keep
    small = small_flow()
    next(small)
    for kind, layer in (("ffn", 1), ("ffn", 0), (None, 0)):
        advance("attn", 0, after)
        after = order.take()[-1]
        next(small, None)
        if kind is not None:
            advance(kind, layer, after)
            after = (order.take_slow() or [after])[-1]
    advance("attn", 1, after)
    order.take()
    advance("attn", 1, after)
    after = (order.take_slow() or [after])[-1]
    advance("attn", 0, after)
    after = order.take()[-1]
    advance("attn", 0, after)
    next(small, None)
    gain, bias = summed
    if not tidy:
        for kind in GROUPS:
            both = [results[layer, kind] for layer in range(LAYERS)]
            results[kind] = [jnp.stack(item) for item in zip(*both)]
    grad_query, grad_key, grad_value, grad_mixing = results["attn"]
    grad_gate, grad_up, grad_down = results["ffn"]
    return (
        jnp.stack(outputs),
        jnp.stack(grads),
        gain[:LAYERS],
        grad_query,
        grad_key,
        grad_value,
        grad_mixing,
        bias,
        gain[LAYERS:],
        grad_gate,
        grad_up,
        grad_down,
    )


def solution(mesh):
    tokens = P(None, ("dp", "gy"), "gx")
    wide = P(None, "gx", "gy")
    tall = P(None, "gy", "gx")
    return jax.shard_map(
        body,
        mesh=mesh,
        in_specs=(tokens, tokens, P(None, "dp"), P())
        + (wide, wide, wide, tall, P(), P(), wide, wide, tall),
        out_specs=(tokens, tokens, P(), wide, wide, wide, tall, P(), P(), wide, wide, tall),
        check_vma=False,
    )
```

```python
import functools

import jax
import jax.numpy as jnp
from jax import lax
from jax.experimental import pallas as pl
from jax.experimental.pallas import tpu as pltpu
from jax.sharding import PartitionSpec as P

D = 2048
H = 32
DH = 64
NB = 32
LAYERS = 2
MICRO = 2
LEN = 1024
TILE = 256
NEAR = 5
NEG = -1000000000.0
HIGH = lax.Precision.HIGHEST
ROWS = 256
GELU_A = 0.7978845608028654
GELU_B = 0.044715


def lanes_of(head, heads):
    wide = min(2, heads) * DH
    start = head * DH // wide * wide
    return slice(start, start + wide)


def pick(values, head, heads):
    values = values[:, lanes_of(head, heads)]
    if heads == 1:
        return values
    lane = lax.broadcasted_iota(jnp.int32, values.shape, 1)
    return jnp.where((lane // DH) == head % 2, values, jnp.zeros_like(values))


def join(rows, heads):
    if heads == 1:
        return rows[0]
    return jnp.concatenate([rows[h][h % 2 * DH : h % 2 * DH + DH] for h in range(heads)], 0)


def nt(a, b):
    return lax.dot_general(a, b, (((1,), (1,)), ((), ())), preferred_element_type=jnp.float32)


def nn(a, b):
    return lax.dot_general(a, b, (((1,), (0,)), ((), ())), preferred_element_type=jnp.float32)


def build_bias(heads, w_ref, bias):
    for h in range(heads):
        for d in range(NEAR):
            wide = jnp.broadcast_to(w_ref[h, d : d + 1, :], (TILE, 2 * TILE))
            if 0 < d < NEAR - 1:
                wide = pltpu.roll(wide, 0, 1, stride=1, stride_axis=0)
            bias[h, d] = wide[:, :TILE]


def fwd_kernel(heads, span, segr, segc, q_ref, k_ref, v_ref, w_ref, o_ref, lse_ref, bias, turned):
    iq = pl.program_id(0)

    @pl.when(iq == 0)
    def _():
        build_bias(heads, w_ref, bias)
        turned[...] = v_ref[...].T

    q = q_ref[...]
    row_seg = segr[...]
    queries = [pick(q, h, heads) for h in range(heads)]
    wide = min(2, heads) * DH

    def step(kc, carry):
        rows = pl.ds(pl.multiple_of(kc * TILE, TILE), TILE)
        near = jnp.clip(kc - iq + 2, 0, NEAR - 1)
        allowed = segc[rows, :] == row_seg
        k = k_ref[rows, :]
        out = []
        for h in range(heads):
            high, total, acc = carry[h]
            s = nt(k[:, lanes_of(h, heads)], queries[h]) + bias[h, near]
            s = jnp.where(allowed, s, NEG)
            top = jnp.maximum(high, jnp.max(s, axis=0, keepdims=True))
            scale = jnp.exp(high - top)
            e = jnp.exp(s - top)
            total = total * scale + jnp.sum(e, axis=0, keepdims=True)
            acc = acc * scale + nn(turned[lanes_of(h, heads), rows], e.astype(jnp.bfloat16))
            out.append((top, total, acc))
        return tuple(out)

    start = (
        jnp.full((1, TILE), 2 * NEG, jnp.float32),
        jnp.zeros((1, TILE), jnp.float32),
        jnp.zeros((wide, TILE), jnp.float32),
    )
    done = lax.fori_loop(span[0, iq], span[1, iq], step, (start,) * heads)
    lse_ref[...] = jnp.zeros_like(lse_ref)
    for h in range(heads):
        lse_ref[h : h + 1, :] = done[h][0] + jnp.log(done[h][1])
    out = join([acc / total for _, total, acc in done], heads)
    o_ref[...] = out.T.astype(o_ref.dtype)


def bwd_kernel(
    heads,
    span,
    segr,
    segc,
    q_ref,
    k_ref,
    v_ref,
    w_ref,
    o_ref,
    lse_ref,
    go_ref,
    gq_ref,
    gk_ref,
    gv_ref,
    gb_ref,
    bias,
    gbias,
    gk_acc,
    gv_acc,
    turned,
):
    iq = pl.program_id(0)

    @pl.when(iq == 0)
    def _():
        build_bias(heads, w_ref, bias)
        turned[...] = k_ref[...].T
        gbias[...] = jnp.zeros_like(gbias)
        gk_acc[...] = jnp.zeros_like(gk_acc)
        gv_acc[...] = jnp.zeros_like(gv_acc)

    q = q_ref[...]
    go = go_ref[...]
    row_seg = segr[...]
    prod = (o_ref[...].astype(jnp.float32) * go.astype(jnp.float32)).T
    queries = [pick(q, h, heads) for h in range(heads)]
    outs = [pick(go, h, heads) for h in range(heads)]
    lse = [lse_ref[h : h + 1, :] for h in range(heads)]
    delta = [
        jnp.sum(prod[h * DH : (h + 1) * DH, :], axis=0, keepdims=True) for h in range(heads)
    ]
    wide = min(2, heads) * DH

    def step(kc, carry):
        rows = pl.ds(pl.multiple_of(kc * TILE, TILE), TILE)
        near = jnp.clip(kc - iq + 2, 0, NEAR - 1)
        allowed = segc[rows, :] == row_seg
        k = k_ref[rows, :]
        v = v_ref[rows, :]
        result = []
        for h in range(heads):
            lanes = lanes_of(h, heads)
            s = nt(k[:, lanes], queries[h]) + bias[h, near]
            s = jnp.where(allowed, s, NEG)
            p = jnp.exp(s - lse[h])
            gp = nt(v[:, lanes], outs[h])
            gs = (p * (gp - delta[h])).astype(jnp.bfloat16)
            gv_acc[rows, lanes] += nn(p.astype(jnp.bfloat16), outs[h])
            gk_acc[rows, lanes] += nn(gs, queries[h])
            gbias[h, near] += gs.astype(jnp.float32)
            result.append(carry[h] + nn(turned[lanes, rows], gs))
        return tuple(result)

    start = (jnp.zeros((wide, TILE), jnp.float32),) * heads
    done = lax.fori_loop(span[0, iq], span[1, iq], step, start)
    gq_ref[...] = join(done, heads).T.astype(gq_ref.dtype)

    @pl.when(iq == pl.num_programs(0) - 1)
    def _():
        gk_ref[...] = gk_acc[...].astype(gk_ref.dtype)
        gv_ref[...] = gv_acc[...].astype(gv_ref.dtype)
        gb_ref[...] = jnp.zeros_like(gb_ref)
        down = lax.broadcasted_iota(jnp.int32, (TILE, TILE), 0)
        across = lax.broadcasted_iota(jnp.int32, (TILE, TILE), 1)
        flip = (down + across == TILE - 1).astype(jnp.float32)
        for h in range(heads):
            for d in range(NEAR):
                tile = gbias[h, d]
                if 0 < d < NEAR - 1:
                    tile = lax.dot_general(
                        flip,
                        tile,
                        (((1,), (0,)), ((), ())),
                        precision=HIGH,
                        preferred_element_type=jnp.float32,
                    )
                wide = jnp.concatenate([tile, jnp.zeros_like(tile)], axis=1)
                if 0 < d < NEAR - 1:
                    wide = pltpu.roll(wide, 0, 1, stride=1, stride_axis=0)
                gb_ref[h, d : d + 1, :] = jnp.sum(wide, axis=0, keepdims=True)


def parts_of(qkv, width):
    if width % 128 == 0:
        return [(qkv, n) for n in range(3)]
    return [(qkv[:, n * width : (n + 1) * width], 0) for n in range(3)]


def seen_specs(qkv, heads):
    width = heads * DH
    (qa, q0), (ka, k0), (va, v0) = parts_of(qkv, width)
    specs = [
        pl.BlockSpec((1, TILE), lambda i, s: (0, i)),
        pl.BlockSpec((LEN, 1), lambda i, s: (0, 0)),
        pl.BlockSpec((TILE, width), lambda i, s: (i, q0)),
        pl.BlockSpec((LEN, width), lambda i, s: (0, k0)),
        pl.BlockSpec((LEN, width), lambda i, s: (0, v0)),
        pl.BlockSpec((heads, NEAR, 2 * TILE), lambda i, s: (0, 0, 0)),
    ]
    return specs, (qa, ka, va)


def attend(qkv, span, segr, segc, w):
    heads = w.shape[0]
    width = heads * DH
    specs, parts = seen_specs(qkv, heads)
    tile = pl.BlockSpec((TILE, width), lambda i, s: (i, 0))
    sums = pl.BlockSpec((8, TILE), lambda i, s: (0, i))
    grid = pltpu.PrefetchScalarGridSpec(
        num_scalar_prefetch=1,
        grid=(LEN // TILE,),
        in_specs=specs,
        out_specs=[tile, sums],
        scratch_shapes=[
            pltpu.VMEM((heads, NEAR, TILE, TILE), jnp.float32),
            pltpu.VMEM((width, LEN), jnp.bfloat16),
        ],
    )
    return pl.pallas_call(
        functools.partial(fwd_kernel, heads),
        grid_spec=grid,
        out_shape=[
            jax.ShapeDtypeStruct((LEN, width), jnp.bfloat16),
            jax.ShapeDtypeStruct((8, LEN), jnp.float32),
        ],
        compiler_params=pltpu.CompilerParams(vmem_limit_bytes=40 * 1024 * 1024),
        cost_estimate=pl.CostEstimate(flops=0, bytes_accessed=0, transcendentals=0),
    )(span, segr, segc, *parts, w)


def bwd_waiting(heads, waits, *refs):
    bwd_kernel(heads, *refs[:10], *refs[10 + waits :])


def attend_back(qkv, span, segr, segc, w, o, lse, go, after):
    heads = w.shape[0]
    width = heads * DH
    specs, parts = seen_specs(qkv, heads)
    tile = pl.BlockSpec((TILE, width), lambda i, s: (i, 0))
    sums = pl.BlockSpec((8, TILE), lambda i, s: (0, i))
    whole = pl.BlockSpec((LEN, width), lambda i, s: (0, 0))
    grid = pltpu.PrefetchScalarGridSpec(
        num_scalar_prefetch=1,
        grid=(LEN // TILE,),
        in_specs=specs + [tile, sums, tile] + [pl.BlockSpec(memory_space=pl.ANY)] * len(after),
        out_specs=[tile, whole, whole, pl.BlockSpec((heads, 8, 2 * TILE), lambda i, s: (0, 0, 0))],
        scratch_shapes=[pltpu.VMEM((heads, NEAR, TILE, TILE), jnp.float32)] * 2
        + [pltpu.VMEM((LEN, width), jnp.float32)] * 2
        + [pltpu.VMEM((width, LEN), jnp.bfloat16)],
    )
    flat = jax.ShapeDtypeStruct((LEN, width), jnp.bfloat16)
    return pl.pallas_call(
        functools.partial(bwd_waiting, heads, len(after)),
        grid_spec=grid,
        out_shape=[flat, flat, flat, jax.ShapeDtypeStruct((heads, 8, 2 * TILE), jnp.float32)],
        compiler_params=pltpu.CompilerParams(vmem_limit_bytes=40 * 1024 * 1024),
        cost_estimate=pl.CostEstimate(flops=0, bytes_accessed=0, transcendentals=0),
    )(span, segr, segc, *parts, w, o, lse, go, *after)


THRESHOLDS = (12, 16, 23, 32, 46, 64, 91)
def bucket_of(offset):
    distance = jnp.abs(offset)
    beyond = 8 + sum(((distance >= threshold).astype(jnp.int32) for threshold in THRESHOLDS))
    within = jnp.where(distance < 8, distance, beyond)
    return jnp.where(offset > 0, 16, 0) + within

def near_table(back):
    place = jnp.arange(2*TILE, dtype=jnp.int32)
    turn = place - (TILE - 1) if back else jnp.where(place < TILE, place, place - 2*TILE)
    offset = TILE*(jnp.arange(NEAR, dtype=jnp.int32) - 2)[:, None] - turn[None, :]
    return (bucket_of(offset)[:, :, None] == jnp.arange(NB, dtype=jnp.int32)).astype(jnp.float32)

def segment_views(segment):
    places = jnp.arange(LEN, dtype=jnp.int32)
    own = jnp.where(segment == 0, 4 + places, segment)
    order = jnp.where(segment == 0, 4, segment).reshape(-1, TILE)
    low, high = order[:, 0], order[:, -1]
    lo = jnp.sum((high[None, :] < low[:, None]).astype(jnp.int32), axis=1)
    hi = jnp.sum((low[None, :] <= high[:, None]).astype(jnp.int32), axis=1)
    return jnp.stack((lo, hi)), own[None, :], own[:, None]


NN = ((1,), (0,))
NT = ((1,), (1,))
TN = ((0,), (0,))
BF = jnp.bfloat16
F32 = jnp.float32


def core_swap(values):
    return lax.ppermute(values, "gx", [(0, 1), (1, 0)])


def token_gather(values):
    return lax.all_gather(values, "gy", axis=0, tiled=True)


def token_reduce(values):
    return lax.psum_scatter(values, "gy", scatter_dimension=0, tiled=True).astype(F32)


def shifted(values, step):
    size = lax.axis_size("gy")
    return lax.ppermute(values, "gy", [(n, (n + step) % size) for n in range(size)])


def dot(left, right, dims):
    return lax.dot_general(left, right, (dims, ((), ())), preferred_element_type=F32)


def rows_kernel(dims, count, extras, waits, finish, *refs):
    total = None
    for n in range(count):
        part = dot(refs[n][...], refs[count + n][...], dims)
        total = part if total is None else total + part
    inner = 2 * count + extras
    finish(total, [ref[...] for ref in refs[2 * count : inner]], refs[inner + waits :])


def keep_rounded(total, extras, outs):
    outs[0][...] = total.astype(BF)


def add_rounded(total, extras, outs):
    outs[0][...] = (total + extras[0].astype(F32)).astype(BF)


def gelu_parts(gate):
    inner = GELU_A * (gate + GELU_B * gate * gate * gate)
    half = 0.5 * (1.0 + jnp.tanh(inner))
    return half, gate * half


def gate_rounded(total, extras, outs):
    total = total + extras[0].astype(F32)
    width = total.shape[1] // 2
    gate, up = total[:, :width], total[:, width:]
    outs[0][...] = total.astype(BF)
    outs[1][...] = (gelu_parts(gate)[1] * up).astype(BF)


def gate_back_rounded(total, extras, outs):
    grad = total + extras[0].astype(F32)
    width = grad.shape[1]
    gate = extras[1][:, :width].astype(F32)
    up = extras[1][:, width:].astype(F32)
    half, value = gelu_parts(gate)
    slope = half + 2.0 * gate * half * (1.0 - half) * GELU_A * (1.0 + 3.0 * GELU_B * gate * gate)
    outs[0][:, :width] = (grad * up * slope).astype(BF)
    outs[0][:, width:] = (grad * value).astype(BF)


def rows_dot(parts, weights, dims, finish=keep_rounded, extras=(), widths=None, after=()):
    rows = parts[0].shape[0]
    if widths is None:
        widths = (weights[0].shape[1 - dims[1][0]],)
    outs = [jax.ShapeDtypeStruct((rows, width), BF) for width in widths]
    if not all(item.shape[1] % 128 == 0 for item in (*parts, *weights, *extras, *outs)):
        return plain_dot(parts, weights, dims, finish, extras, outs)
    tall = min(rows, ROWS)

    def sliced(item):
        return pl.BlockSpec((tall, item.shape[1]), lambda i: (i, 0))

    def whole(item):
        return pl.BlockSpec(item.shape, lambda i: (0, 0))

    result = pl.pallas_call(
        functools.partial(rows_kernel, dims, len(parts), len(extras), len(after), finish),
        grid=(rows // tall,),
        in_specs=[sliced(item) for item in parts]
        + [whole(item) for item in weights]
        + [sliced(item) for item in extras]
        + [pl.BlockSpec(memory_space=pl.ANY)] * len(after),
        out_specs=[sliced(item) for item in outs],
        out_shape=outs,
        compiler_params=pltpu.CompilerParams(vmem_limit_bytes=40 * 1024 * 1024),
        cost_estimate=pl.CostEstimate(flops=0, bytes_accessed=0, transcendentals=0),
    )(*parts, *weights, *extras, *after)
    return result[0] if len(outs) == 1 else result


def join_kernel(count, waits, *refs):
    width = refs[0].shape[1]
    for n in range(count):
        refs[count + waits][:, n * width : (n + 1) * width] = refs[n][...]


def rows_join(parts, after):
    rows, width = parts[0].shape
    count = len(parts)
    if width % 128:
        return jnp.concatenate(parts, 1)
    tall = min(rows, ROWS)
    return pl.pallas_call(
        functools.partial(join_kernel, count, len(after)),
        grid=(rows // tall,),
        in_specs=[pl.BlockSpec((tall, width), lambda i: (i, 0))] * count
        + [pl.BlockSpec(memory_space=pl.ANY)] * len(after),
        out_specs=pl.BlockSpec((tall, count * width), lambda i: (i, 0)),
        out_shape=jax.ShapeDtypeStruct((rows, count * width), BF),
        compiler_params=pltpu.CompilerParams(vmem_limit_bytes=40 * 1024 * 1024),
        cost_estimate=pl.CostEstimate(flops=0, bytes_accessed=0, transcendentals=0),
    )(*parts, *after)


def grads_kernel(groups, micros, waits, blocks, mine, *refs):
    kept, sent = refs[-2:]
    ours = (pl.program_id(0) // blocks) == mine[0]
    rights = sum(groups)
    each = len(groups) + rights
    column = 0
    for g, size in enumerate(groups):
        turned = [refs[n * each + g][...].T for n in range(micros)]
        first = len(groups) + sum(groups[:g])
        for j in range(first, first + size):
            total = sum(dot(turned[n], refs[n * each + j][...], NN) for n in range(micros))
            total = total.astype(BF)
            place = slice(column, column + total.shape[1])
            column = place.stop

            @pl.when(ours)
            def _():
                kept[:, place] = total

            @pl.when(jnp.logical_not(ours))
            def _():
                sent[:, place] = total


def half_spec(rows, width, blocks, ours):
    def index(i, s):
        which = s[0] if ours else 1 - s[0]
        return jnp.clip(i - which * blocks, 0, blocks - 1), 0

    return pl.BlockSpec((rows, width), index)


def local_call(kernel, scalar, grid, in_specs, out_specs, out_shape, arrays, after):
    spec = pltpu.PrefetchScalarGridSpec(
        num_scalar_prefetch=1,
        grid=grid,
        in_specs=in_specs + [pl.BlockSpec(memory_space=pl.ANY)] * len(after),
        out_specs=out_specs,
    )
    return pl.pallas_call(
        kernel,
        grid_spec=spec,
        out_shape=out_shape,
        compiler_params=pltpu.CompilerParams(vmem_limit_bytes=56 * 1024 * 1024),
        cost_estimate=pl.CostEstimate(flops=0, bytes_accessed=0, transcendentals=0),
    )(scalar.astype(jnp.int32).reshape(1), *arrays, *after)


def packed_grads(items, mine, after):
    groups = [len(rights) for _, rights in items[0]]
    depth = items[0][0][0].shape[1]
    if any(right.shape[1] % 128 for _, rights in items[0] for right in rights):
        result = []
        for g, size in enumerate(groups):
            for j in range(size):
                parts = [dot(item[g][0], item[g][1][j], TN) for item in items]
                result.append(sum(parts).astype(BF))
        total = jnp.concatenate(result, 1)
        return take_half(total, mine), take_half(total, 1 - mine)
    arrays, specs = [], []
    for item in items:
        for left, _ in item:
            arrays.append(left)
            specs.append(pl.BlockSpec((left.shape[0], ROWS), lambda i, s: (0, i)))
        for _, rights in item:
            arrays.extend(rights)
            specs.extend(pl.BlockSpec(right.shape, lambda i, s: (0, 0)) for right in rights)
    width = sum(right.shape[1] for _, rights in items[0] for right in rights)
    blocks = depth // ROWS // 2
    return local_call(
        functools.partial(grads_kernel, groups, len(items), len(after), blocks),
        mine,
        (2 * blocks,),
        specs,
        [half_spec(ROWS, width, blocks, ours) for ours in (True, False)],
        [jax.ShapeDtypeStruct((depth // 2, width), BF)] * 2,
        arrays,
        after,
    )


def halve_kernel(waits, blocks, mine, have, come, *refs):
    kept, sent = refs[waits:]
    total = (have[...].astype(F32) + come[...].astype(F32)).astype(BF)
    ours = (pl.program_id(0) // blocks) == mine[0]

    @pl.when(ours)
    def _():
        kept[...] = total

    @pl.when(jnp.logical_not(ours))
    def _():
        sent[...] = total


def halve(have, come, mine, after):
    rows, width = have.shape
    if width % 128 or rows % 64:
        total = (have.astype(F32) + come.astype(F32)).astype(BF)
        return take_half(total, mine), take_half(total, 1 - mine)
    tall = rows // 4
    return local_call(
        functools.partial(halve_kernel, len(after), 2),
        mine,
        (4,),
        [pl.BlockSpec((tall, width), lambda i, s: (i, 0))] * 2,
        [half_spec(tall, width, 2, ours) for ours in (True, False)],
        [jax.ShapeDtypeStruct((rows // 2, width), BF)] * 2,
        [have, come],
        after,
    )


def total_kernel(waits, mine, have, come, *refs):
    refs[waits][...] = (have[...].astype(F32) + come[...].astype(F32)).astype(BF)


def double_kernel(waits, blocks, mine, own, come, *refs):
    ours = (pl.program_id(0) // blocks) == mine[0]

    @pl.when(ours)
    def _():
        refs[waits][...] = own[...]

    @pl.when(jnp.logical_not(ours))
    def _():
        refs[waits][...] = come[...]


def arrive_kernel(*refs):
    refs[-1][...] = jnp.zeros_like(refs[-1])


def arrived(come, after):
    return pl.pallas_call(
        arrive_kernel,
        in_specs=[pl.BlockSpec(memory_space=pl.ANY)] * (1 + len(after)),
        out_shape=jax.ShapeDtypeStruct((8, 128), F32),
        cost_estimate=pl.CostEstimate(flops=0, bytes_accessed=0, transcendentals=0),
    )(come, *after)


def total_of(have, come, mine, after):
    rows, width = have.shape
    if width % 128 or rows % 32:
        return (have.astype(F32) + come.astype(F32)).astype(BF)
    tall = rows // 2
    spec = pl.BlockSpec((tall, width), lambda i, s: (i, 0))
    shape = jax.ShapeDtypeStruct((rows, width), BF)
    kernel = functools.partial(total_kernel, len(after))
    return local_call(kernel, mine, (2,), [spec] * 2, spec, shape, [have, come], after)


def double(own, come, mine, after):
    rows, width = own.shape
    if width % 128 or rows % 32:
        return stack_half(own, come, mine)
    tall = rows // 2
    return local_call(
        functools.partial(double_kernel, len(after), 2),
        mine,
        (4,),
        [half_spec(tall, width, 2, ours) for ours in (True, False)],
        pl.BlockSpec((tall, width), lambda i, s: (i, 0)),
        jax.ShapeDtypeStruct((2 * rows, width), BF),
        [own, come],
        after,
    )


class Holder:
    def __init__(self, shape):
        self.value = jnp.zeros(shape.shape, shape.dtype)

    def __setitem__(self, place, value):
        self.value = value if place is Ellipsis else self.value.at[place].set(value)


def plain_dot(parts, weights, dims, finish, extras, outs):
    total = sum(dot(part, weight, dims) for part, weight in zip(parts, weights))
    held = [Holder(item) for item in outs]
    finish(total, extras, held)
    return held[0].value if len(held) == 1 else [item.value for item in held]


def row_norm(hidden):
    part = jnp.sum(hidden * hidden, axis=1)
    return lax.rsqrt((part + core_swap(part)) / D + 1e-06)


def norm_back(grad_norm, hidden, scale, gain):
    weighted = grad_norm * gain
    part = jnp.sum(weighted * hidden, axis=1)
    inner = part + core_swap(part)
    cubed = scale * scale * scale * inner / D
    grad_hidden = scale[:, None] * weighted - hidden * cubed[:, None]
    gain_grad = jnp.sum(grad_norm * hidden * scale[:, None], axis=0)
    return grad_hidden, gain_grad


def halves(weights, axis, core):
    width = weights.shape[axis] // 2
    own = lax.dynamic_slice_in_dim(weights, core * width, width, axis)
    other = lax.dynamic_slice_in_dim(weights, (1 - core) * width, width, axis)
    return own, other


def in_order(own, other, core, axis):
    return jnp.where(
        core == 0,
        jnp.concatenate((own, other), axis),
        jnp.concatenate((other, own), axis),
    )


def paired(*weights):
    cut = [jnp.split(item, 2, axis=1) for item in weights]
    return jnp.concatenate([item[n] for n in range(2) for item in cut], 1)


def link_swap(values, bits):
    size = lax.axis_size("dp")
    pairs = [(n * 2 + c, (n ^ bits[c]) * 2 + c) for n in range(size) for c in range(2)]
    return lax.ppermute(values, ("dp", "gx"), pairs)


def take_half(values, which):
    rows = values.shape[0] // 2
    return lax.dynamic_slice_in_dim(values, which * rows, rows, 0)


def stack_half(own, other, which):
    return jnp.where(
        which == 0,
        jnp.concatenate((own, other), 0),
        jnp.concatenate((other, own), 0),
    )


def batch_steps(place, core):
    size = lax.axis_size("dp")
    bits = [1 << n for n in range(size.bit_length() - 1)]
    steps = []
    for first, second in zip(bits, bits[::-1]):
        bit = jnp.where(core == 0, first, second)
        steps.append(((first, second), jnp.where((place & bit) != 0, 1, 0)))
    return steps


def settle_kernel(count, waits, blocks, place, own_ref, other_ref, *refs):
    outs = refs[waits:]
    half = pl.program_id(0) // blocks

    def store(values, core):
        width = outs[0].shape[2] // 2
        tall = outs[count].shape[1] // 2
        for part in range(2):
            spot = part ^ core
            for n in range(count):
                start = (part * count + n) * width
                cut = values[:, start : start + width].astype(F32)
                outs[n][0, :, spot * width : (spot + 1) * width] = cut
            start = 2 * count * width + part * tall
            cut = values[:, start : start + tall].astype(F32)
            outs[count][0, spot * tall : (spot + 1) * tall, :] = cut.T

    for source, ref in enumerate((own_ref, other_ref)):
        for core in range(2):

            @pl.when(((half ^ place[0]) == source) & (place[1] == core))
            def _():
                store(ref[...], core)


def settle(own, other, flag, core, layer, targets, shapes, after):
    rows = 128
    blocks = own.shape[0] // rows

    def block(source):
        def index(i, s):
            return jnp.where(((i // blocks) ^ s[0]) == source, i % blocks, 0), 0

        return pl.BlockSpec((rows, own.shape[1]), index)

    count = len(shapes) - 1
    grid = pltpu.PrefetchScalarGridSpec(
        num_scalar_prefetch=1,
        grid=(2 * blocks,),
        in_specs=[block(0), block(1)]
        + [pl.BlockSpec(memory_space=pl.ANY)] * (len(targets) + len(after)),
        out_specs=[
            pl.BlockSpec((1, rows, item.shape[2]), lambda i, s: (layer, i, 0))
            for item in shapes[:count]
        ]
        + [pl.BlockSpec((1, shapes[count].shape[1], rows), lambda i, s: (layer, 0, i))],
    )
    return pl.pallas_call(
        functools.partial(settle_kernel, count, len(targets) + len(after), blocks),
        grid_spec=grid,
        out_shape=shapes,
        input_output_aliases={3 + n: n for n in range(len(targets))},
        compiler_params=pltpu.CompilerParams(vmem_limit_bytes=40 * 1024 * 1024),
        cost_estimate=pl.CostEstimate(flops=0, bytes_accessed=0, transcendentals=0),
    )(jnp.stack((flag, core)).astype(jnp.int32), own, other, *targets, *after)


def plain_settle(values, core, shapes):
    count = len(shapes) - 1
    width = shapes[0].shape[2] // 2
    cut = [values[:, n * width : (n + 1) * width] for n in range(2 * count)]
    done = [in_order(cut[n], cut[count + n], core, 1) for n in range(count)]
    own, other = jnp.split(values[:, 2 * count * width :].T, 2, 0)
    return done + [in_order(own, other, core, 0)]


def axis_sum(values, axis):
    size = lax.axis_size(axis)

    def swapped(item, bits):
        return lax.ppermute(item, axis, [(n, n ^ bits) for n in range(size)])

    if size == 4:
        one, two, three = (swapped(values, bits) for bits in (1, 2, 3))
        return (values + one) + (two + three)
    bit = 1
    while bit < size:
        values = values + swapped(values, bit)
        bit *= 2
    return values


GROUPS = ("ffn", "attn")


class Order:
    def __init__(self):
        self.last = None
        self.dues = []
        self.slow = []
        self.gate = []

    def enter(self, *values):
        if self.last is None:
            return values
        return lax.optimization_barrier((*values, self.last))[:-1]

    def leave(self, value):
        self.last = value

    def due(self, value):
        self.dues.append(value)

    def take(self):
        dues, self.dues = self.dues, []
        return dues

    def take_slow(self):
        dues, self.slow = self.slow, []
        return dues


def body(
    inputs,
    cotangent,
    segments,
    attention_gain,
    query_weight,
    key_weight,
    value_weight,
    mixing_weight,
    relative_bias,
    dense_gain,
    gate_weight,
    up_weight,
    down_weight,
):
    core = lax.axis_index("gx")
    block = lax.axis_index("gy")
    place = lax.axis_index("dp")
    row_count = inputs.shape[1]
    col_count = inputs.shape[2]
    col_start = core * col_count
    heads_dev = query_weight.shape[2] // (2 * DH)
    head_start = (block * 2 + core) * heads_dev
    hidden_dev = gate_weight.shape[2] // 2
    ahead = near_table(False)
    behind = near_table(True)
    steps = batch_steps(place, core)
    order = Order()
    later = {}
    flows = {}
    summed = []
    ends = []
    results = {}
    tidy = hidden_dev % 128 == 0 and (heads_dev * DH) % 128 == 0
    shapes = {
        kind: [jax.ShapeDtypeStruct(item.shape, F32) for item in group]
        for kind, group in (
            ("attn", (query_weight, key_weight, value_weight, mixing_weight)),
            ("ffn", (gate_weight, up_weight, down_weight)),
        )
    }
    layers = []
    for layer in range(LAYERS):
        qkv = paired(query_weight[layer], key_weight[layer], value_weight[layer])
        gu = paired(gate_weight[layer], up_weight[layer])
        table = lax.dynamic_slice_in_dim(relative_bias[layer], head_start, heads_dev, 1)
        layers.append(
            dict(
                qkv_half=halves(qkv, 1, core),
                gu_half=halves(gu, 1, core),
                mix_half=halves(mixing_weight[layer], 0, core),
                down_half=halves(down_weight[layer], 0, core),
                bias=jnp.einsum("dcb,bh->hdc", ahead, table, precision=HIGH),
                gain1=lax.dynamic_slice_in_dim(attention_gain[layer], col_start, col_count),
                gain2=lax.dynamic_slice_in_dim(dense_gain[layer], col_start, col_count),
            )
        )
    acc = [dict() for _ in range(LAYERS)]

    def add(layer, name, value):
        have = acc[layer].get(name)
        acc[layer][name] = value if have is None else have + value

    def batch_flow(layer, kind, kept, sent):
        (bits1, mine1), (bits2, mine2) = steps
        come = link_swap(sent, bits1)
        yield
        kept, sent = halve(kept, come, mine2, order.gate)
        order.due(kept)
        come = link_swap(sent, bits2)
        yield
        kept = total_of(kept, come, mine2, order.gate)
        order.due(kept)
        come = link_swap(kept, bits2)
        yield
        kept = double(kept, come, mine2, order.gate)
        order.due(kept)
        come = link_swap(kept, bits1)
        yield
        order.due(arrived(come, order.gate))
        yield
        if tidy:
            targets = results.get(kind, [])
            results[kind] = settle(
                kept, come, mine1, core, layer, targets, shapes[kind], order.gate
            )
            order.slow.append(results[kind][0])
        else:
            kept = stack_half(kept, come, mine1).astype(F32)
            results[layer, kind] = plain_settle(kept, core, shapes[kind])

    def small_flow():
        gain = jnp.stack([acc[n][name] for name in ("gain1", "gain2") for n in range(LAYERS)])
        gain = lax.dynamic_update_slice_in_dim(jnp.zeros((2 * LAYERS, D), F32), gain, col_start, 1)
        bias = jnp.stack([acc[n]["bias"][:, :NEAR] for n in range(LAYERS)])
        bias = jnp.einsum("lhdc,dcb->lbh", bias, behind, precision=HIGH)
        bias = lax.dynamic_update_slice_in_dim(
            jnp.zeros((LAYERS, NB, H), F32), bias, head_start, 2
        )
        total = jnp.concatenate((gain.reshape(-1, 128), bias.reshape(-1, 128)), 0)
        for axis in ("gx", "gy", "dp"):
            total = axis_sum(total, axis)
            yield
        split = gain.size // 128
        summed.append(total[:split].reshape(gain.shape))
        summed.append(total[split:].reshape(bias.shape))

    def weight_grads():
        for (layer, kind), items in list(later.items()):
            if len(items) == MICRO:
                before = order.last
                if kind == "ffn":
                    advance("attn", layer + 1)
                kept, sent = packed_grads(items, steps[0][1], [before, *order.take()])
                order.leave(kept)
                flow = batch_flow(layer, kind, kept, sent)
                next(flow)
                flows[kind, layer] = flow
                del later[layer, kind]

    def advance(kind, layer, gate=None):
        order.gate = [order.last if gate is None else gate]
        if (kind, layer) in flows and next(flows[kind, layer], "end") == "end":
            del flows[kind, layer]

    def forward(micro):
        seg_all = segments[micro]
        row_segs = lax.dynamic_slice_in_dim(seg_all, block * row_count, row_count)
        keep = (row_segs != 0).astype(F32)[:, None]
        views = segment_views(seg_all)
        hidden = inputs[micro].astype(F32)
        saved = []
        for layer in range(LAYERS):
            w = layers[layer]
            scale1 = row_norm(hidden)
            normed = (hidden * scale1[:, None] * w["gain1"]).astype(BF)
            order.leave(normed)
            normed = token_gather(normed)
            yield
            (normed,) = order.enter(normed)
            come = core_swap(rows_dot([normed], w["qkv_half"][1:], NN))
            qkv = rows_dot([normed], w["qkv_half"][:1], NN, add_rounded, [come])
            own, lse = attend(qkv, *views, w["bias"])
            mixed = [own, core_swap(own)]
            branch = rows_dot(mixed, w["mix_half"], NN)
            order.leave(branch)
            branch = token_reduce(branch)
            yield
            (branch,) = order.enter(branch)
            middle = hidden + branch
            scale2 = row_norm(middle)
            dense = (middle * scale2[:, None] * w["gain2"]).astype(BF)
            order.leave(dense)
            dense = token_gather(dense)
            yield
            (dense,) = order.enter(dense)
            come = core_swap(rows_dot([dense], w["gu_half"][1:], NN))
            gate_up, active = rows_dot(
                [dense],
                w["gu_half"][:1],
                NN,
                gate_rounded,
                [come],
                (2 * hidden_dev, hidden_dev),
            )
            active = [active, core_swap(active)]
            saved.append(
                (hidden, scale1, normed, qkv, lse, mixed, middle, scale2, dense)
                + (gate_up, active)
            )
            if layer == LAYERS - 1:
                break
            out = rows_dot(active, w["down_half"], NN)
            order.leave(out)
            out = token_reduce(out)
            yield
            (out,) = order.enter(out)
            hidden = middle + out
        ends.append((middle, active, w["down_half"], keep))
        grad = cotangent[micro].astype(F32) * keep
        for layer in reversed(range(LAYERS)):
            w = layers[layer]
            hidden, scale1, normed, qkv, lse, mixed = saved[layer][:6]
            middle, scale2, dense, gate_up, active = saved[layer][6:]
            grad_out = grad.astype(BF)
            order.leave(grad_out)
            grad_out = token_gather(grad_out)
            yield
            (grad_out,) = order.enter(grad_out)
            if micro == 0:
                advance("ffn", layer + 1)
            advance("attn", layer + 1)
            dues = order.take()
            come = core_swap(rows_dot([grad_out], w["down_half"][1:], NT, after=dues))
            pair = rows_dot(
                [grad_out],
                w["down_half"][:1],
                NT,
                gate_back_rounded,
                [come, gate_up],
                (2 * hidden_dev,),
            )
            pair = [pair, core_swap(pair)]
            grad_dense = rows_dot(pair, w["gu_half"], NT, after=order.take())
            order.leave(grad_dense)
            grad_dense = token_reduce(grad_dense)
            item = [(dense, pair), (grad_out, active)]
            later.setdefault((layer, "ffn"), []).append(item)
            yield
            (grad_dense,) = order.enter(grad_dense)
            grad_norm, gain_part = norm_back(grad_dense, middle, scale2, w["gain2"])
            add(layer, "gain2", gain_part)
            grad_mid = grad + grad_norm
            grad_out = grad_mid.astype(BF)
            order.leave(grad_out)
            grad_out = token_gather(grad_out)
            yield
            (grad_out,) = order.enter(grad_out)
            if micro == 0:
                advance("ffn", layer)
            elif layer == 0:
                advance("ffn", layer, grad_out)
            dues = order.take()
            come = core_swap(rows_dot([grad_out], w["mix_half"][1:], NT, after=dues))
            grad_mixed = rows_dot([grad_out], w["mix_half"][:1], NT, add_rounded, [come])
            gq, gk, gv, gb = attend_back(
                qkv, *views, w["bias"], mixed[0], lse, grad_mixed, order.take()
            )
            add(layer, "bias", gb)
            advance("ffn", layer, gq)
            triple = rows_join((gq, gk, gv), order.take())
            triple = [triple, core_swap(triple)]
            grad_normed = rows_dot(triple, w["qkv_half"], NT)
            order.leave(grad_normed)
            grad_normed = token_reduce(grad_normed)
            item = [(normed, triple), (grad_out, mixed)]
            later.setdefault((layer, "attn"), []).append(item)
            yield
            (grad_normed,) = order.enter(grad_normed)
            grad_norm, gain_part = norm_back(grad_normed, hidden, scale1, w["gain1"])
            add(layer, "gain1", gain_part)
            grad = grad_mid + grad_norm
        grads[micro] = grad

    outputs = [None] * MICRO
    grads = [None] * MICRO
    micro_flows = [forward(micro) for micro in range(MICRO)]
    live = list(micro_flows)
    while live:
        for flow in list(live):
            if next(flow, "end") == "end":
                live.remove(flow)
        weight_grads()
    after = [order.last, *order.take()]
    last = [rows_dot(active, down, NN, after=after) for _, active, down, _ in ends]
    after = last[-1]
    last = jnp.split(token_reduce(jnp.concatenate(last, 1)), MICRO, 1)
    for n, (middle, _, _, keep) in enumerate(ends):
        outputs[n] = (middle + last[n]) * keep
    small = small_flow()
    next(small)
    for kind, layer in (("ffn", 1), ("ffn", 0), (None, 0)):
        advance("attn", 0, after)
        after = order.take()[-1]
        next(small, None)
        if kind is not None:
            advance(kind, layer, after)
            after = (order.take_slow() or [after])[-1]
    advance("attn", 1, after)
    order.take()
    advance("attn", 1, after)
    after = (order.take_slow() or [after])[-1]
    advance("attn", 0, after)
    after = order.take()[-1]
    advance("attn", 0, after)
    next(small, None)
    gain, bias = summed
    if not tidy:
        for kind in GROUPS:
            both = [results[layer, kind] for layer in range(LAYERS)]
            results[kind] = [jnp.stack(item) for item in zip(*both)]
    grad_query, grad_key, grad_value, grad_mixing = results["attn"]
    grad_gate, grad_up, grad_down = results["ffn"]
    return (
        jnp.stack(outputs),
        jnp.stack(grads),
        gain[:LAYERS],
        grad_query,
        grad_key,
        grad_value,
        grad_mixing,
        bias,
        gain[LAYERS:],
        grad_gate,
        grad_up,
        grad_down,
    )


def solution(mesh):
    tokens = P(None, ("dp", "gy"), "gx")
    wide = P(None, "gx", "gy")
    tall = P(None, "gy", "gx")
    return jax.shard_map(
        body,
        mesh=mesh,
        in_specs=(tokens, tokens, P(None, "dp"), P())
        + (wide, wide, wide, tall, P(), P(), wide, wide, tall),
        out_specs=(tokens, tokens, P(), wide, wide, wide, tall, P(), P(), wide, wide, tall),
        check_vma=False,
    )
```
